256 devices in a mesh: feat: 32 (over z, y), graph: 8 (over x, core).
Axes of the slice: x: 4, y: 4, z: 8, core: 2. Of those that a mesh axis runs over, the one named last changes fastest.
Arguments:
- feats: bfloat16 [768, 131072], P('feat', 'graph'), may hold values from -6 to 6
- front_ids: int32 [8, 8, 4096], P(None, 'graph'), may hold values from 0 to 16383, as said below
- nbr1: int32 [8, 1024, 25], replicated, may hold values from -1 to 32767, as said below
- nbr2: int32 [8, 256, 15], P('graph', 'feat'), may hold values from -1 to 1023, as said below
- w1_self: bfloat16 [768, 512], P('feat'), may hold values from -0.21875 to 0.21875
- w1_neigh: bfloat16 [768, 512], P('feat'), may hold values from -0.21875 to 0.21875
- b1: float32 [512], replicated, may hold values from -3 to 3
- w2_self: bfloat16 [512, 153], replicated, may hold values from -0.25 to 0.25
- w2_neigh: bfloat16 [512, 153], replicated, may hold values from -0.25 to 0.25
- b2: float32 [153], replicated, may hold values from -3 to 3
- dlogits: float32 [8, 256, 153], P('graph', 'feat'), may hold values from -6 to 6
Outputs:
- logits: float32 [8, 256, 153], P('graph', 'feat')
- grad_self: float32 [512, 153], replicated
- grad_neigh: float32 [512, 153], replicated
The draws below stay inside these ranges and needn't reach their ends.
Inputs may be any that keep to these rules, and one draw needn't show every extreme that they name: `front_ids`: local vertex ids within the named shard. `nbr1`: each target has 1 to 25 valid entries, first in its row, then -1. `nbr2`: each target has 1 to 15 valid entries, first in its row, then -1.
All inputs are finite; a program needn't handle non-finite values.
Results may differ from the reference program's by a relative error of at most 0.0032.
Values may be sent and summed in bfloat16 or wider, within the bound.
A program may use at most 64 MiB of HBM per device.

```python
import jax
import jax.numpy as jnp
from jax import lax

F = 768
H = 512
C = 153
VDEV = 16384
FS = 4096
T1 = 1024
T2 = 256
K1 = 25
K2 = 15
MB = 8
V = 131072
FR = 32768


def neighbour_block(key, rows, fan, span):
    deg_key, val_key = jax.random.split(key)
    degree = jax.random.randint(deg_key, (MB, rows), 1, fan + 1, dtype=jnp.int32)
    degree = degree.at[:, 0].set(fan).at[:, 1].set(1)
    values = jax.random.randint(val_key, (MB, rows, fan), 0, span, dtype=jnp.int32)
    values = values.at[0, 0, 0].set(0).at[0, 1, 0].set(span - 1)
    slots = jnp.arange(fan, dtype=jnp.int32)[None, None, :]
    return jnp.where(slots < degree[:, :, None], values, -1).astype(jnp.int32)


def draw_front_ids(key, part):
    key = jax.random.fold_in(key, 11)
    ids = jax.random.randint(key, (MB, MB, FS), 0, VDEV, dtype=jnp.int32)
    return ids.at[0, 0, 0].set(VDEV - 1).at[0, 0, 1].set(0)


def draw_nbr1(key, part):
    key = jax.random.fold_in(key, 12)
    return neighbour_block(key, T1, K1, FR)


def draw_nbr2(key, part):
    key = jax.random.fold_in(key, 13)
    return neighbour_block(key, T2, K2, T1)


def levels(stream_key, dims, shards, smallest, top_value):
    factor_of = 1.0
    for axis_at, shards_of in shards:
        steps = jax.random.uniform(jax.random.fold_in(jax.random.fold_in(stream_key, 6), axis_at), (shards_of,), jnp.float32, smallest / len(shards), top_value / len(shards))
        factor_of = factor_of * jnp.repeat(jnp.exp(steps), dims[axis_at] // shards_of).reshape((-1,) + (1,) * (len(dims) - 1 - axis_at))
    return factor_of


def bell_draw(key, extent, scale, reach, cuts=(), held_as=jnp.bfloat16):
    drawn = jax.random.normal(key, extent, jnp.float32) * scale
    if len(cuts) > 0:
        drawn = levels(key, extent, cuts, -0.22, 0.18) * drawn
    return jnp.clip(drawn, min=-reach, max=reach).astype(held_as)


def setup_inputs(seed: int = 0) -> dict:
    keys = jax.random.split(jax.random.key(seed), 12)
    feats = bell_draw(keys[0], (F, V), 1.0, 6.0, ((0, 32), (1, 8)))
    front_ids = draw_front_ids(jax.random.fold_in(keys[11], 71), 0)
    nbr1 = draw_nbr1(jax.random.fold_in(keys[11], 71), 0)
    nbr2 = draw_nbr2(jax.random.fold_in(keys[11], 71), 0)
    w1_self = bell_draw(keys[4], (F, H), F ** -0.5, 0.21875, ((0, 32),))
    w1_neigh = bell_draw(keys[5], (F, H), F ** -0.5, 0.21875, ((0, 32),))
    b1 = bell_draw(keys[6], (H,), 0.5, 3.0, (), jnp.float32)
    w2_self = bell_draw(keys[7], (H, C), H ** -0.5, 0.25)
    w2_neigh = bell_draw(keys[8], (H, C), H ** -0.5, 0.25)
    b2 = bell_draw(keys[9], (C,), 0.5, 3.0, (), jnp.float32)
    dlogits = bell_draw(keys[10], (MB, T2, C), 1.0, 6.0, ((0, 8), (1, 32)), jnp.float32)
    return {"feats": feats, "front_ids": front_ids, "nbr1": nbr1, "nbr2": nbr2, "w1_self": w1_self, "w1_neigh": w1_neigh, "b1": b1, "w2_self": w2_self, "w2_neigh": w2_neigh, "b2": b2, "dlogits": dlogits}


def reference(feats, front_ids, nbr1, nbr2, w1_self, w1_neigh, b1, w2_self, w2_neigh, b2, dlogits):
    shard_base = (jnp.arange(MB, dtype=jnp.int32) * VDEV)[:, None]

    def one_batch(carry, inputs):
        batch, ids, first, second, cotangent = inputs
        columns = (ids + shard_base).astype(jnp.int32)
        frontier = jnp.take(feats, columns, axis=1).reshape(F, FR)
        own_cols = lax.dynamic_slice_in_dim(frontier, (batch * FS).astype(jnp.int32), T1, 1)
        valid = first >= 0
        degree = jnp.sum(valid, axis=1).astype(jnp.float32)
        picked = jnp.take(frontier, jnp.where(valid, first, 0).T, axis=1)
        summed = jnp.sum(jnp.where(valid.T[None], picked.astype(jnp.float32), jnp.float32(0.0)), axis=1)
        mean_cols = summed / degree[None, :]
        pre = jnp.dot(own_cols.T, w1_self, preferred_element_type=jnp.float32)
        pre = pre + jnp.dot(mean_cols.T, w1_neigh.astype(jnp.float32), precision=lax.Precision.HIGHEST)
        hidden = jnp.maximum(pre + b1, 0.0).astype(jnp.bfloat16)
        valid2 = second >= 0
        degree2 = jnp.sum(valid2, axis=1).astype(jnp.float32)
        picked2 = jnp.take(hidden, jnp.where(valid2, second, 0), axis=0)
        mean2 = jnp.sum(jnp.where(valid2[:, :, None], picked2.astype(jnp.float32), jnp.float32(0.0)), axis=1) / degree2[:, None]
        own2 = hidden[:T2]
        scores = jnp.dot(own2, w2_self, preferred_element_type=jnp.float32)
        scores = scores + jnp.dot(mean2, w2_neigh.astype(jnp.float32), precision=lax.Precision.HIGHEST) + b2
        grad_s = jnp.dot(own2.astype(jnp.float32).T, cotangent, precision=lax.Precision.HIGHEST)
        grad_n = jnp.dot(mean2.T, cotangent, precision=lax.Precision.HIGHEST)
        return (carry[0] + grad_s, carry[1] + grad_n), scores

    start = (jnp.zeros((H, C), jnp.float32), jnp.zeros((H, C), jnp.float32))
    batches = jnp.arange(MB, dtype=jnp.int32)
    grads, logits = lax.scan(one_batch, start, (batches, front_ids, nbr1, nbr2, dlogits))
    return logits, grads[0], grads[1]
```

```python
import functools

import jax
import jax.numpy as jnp
from jax import lax
from jax.experimental import pallas as pl
from jax.experimental.pallas import tpu as pltpu
from jax.sharding import PartitionSpec as P

LANES = 128
FRONT_PAD = 1024
UNROLL = 16
MESH = pl.DeviceIdType.MESH
F32 = jnp.float32
BF16 = jnp.bfloat16
VALID = 1 << 29
RANK_AT = 18


def aligned(index, size):
    return pl.ds(pl.multiple_of(index * size, size), size)


def gather_kernel(
    nb, feats_ref, front_ref, nbr_ref, out_ref, self_ref,
    table, acc, own, one, two, rows_v, front_v, count_v,
    front_s, rows_s, front_i, count_s, sems,
):
    width = feats_ref.shape[0]
    verts = feats_ref.shape[1]
    total = nbr_ref.shape[0]
    per = total // nb
    fan = per // 8
    targets = 8 * LANES
    fs = (front_ref.shape[0] - FRONT_PAD) // nb
    graph = lax.axis_index("graph")

    fetch = pltpu.make_async_copy(front_ref, front_s, sems.at[0])
    fetch.start()

    def turn(i, c):
        block = feats_ref[:, aligned(i, LANES)].astype(F32)
        table[aligned(i, LANES), 0:width] = block.T
        return c

    lax.fori_loop(0, verts // LANES, turn, 0, unroll=4)
    table[verts : verts + 8, :] = jnp.zeros((8, LANES), F32)

    def clear(i, c):
        acc[aligned(i, 64), :] = jnp.zeros((64, LANES), F32)
        return c

    lax.fori_loop(0, nb * targets // 64, clear, 0, unroll=4)
    acc[nb * targets : nb * targets + 8, :] = jnp.zeros((8, LANES), F32)

    below = (
        lax.broadcasted_iota(jnp.int32, (per, per), 0)
        > lax.broadcasted_iota(jnp.int32, (per, per), 1)
    ).astype(F32).astype(BF16)
    sub = lax.broadcasted_iota(jnp.int32, (per, LANES), 0) % 8
    lost = jnp.zeros((1, LANES), jnp.int32)
    for b in range(nb):
        ids = nbr_ref[b * per : (b + 1) * per, :]
        here = (ids // fs == graph) & (ids >= 0)
        gone = jnp.where(here, 0.0, 1.0)
        before = jnp.dot(below, gone.astype(BF16), preferred_element_type=F32)
        rank = before.astype(jnp.int32) + lost
        entry = VALID + rank * (1 << RANK_AT) + (ids % fs + b * fs) * 8 + sub
        one[b * per : (b + 1) * per, :] = jnp.where(here, entry, 0)
        lost = lost + jnp.sum(gone, axis=0, keepdims=True).astype(jnp.int32)
    count = total - lost

    src, dst = one, two
    bits = (total - 1).bit_length()
    block = 64
    for step in range(bits):
        far = 1 << step
        flag = 1 << (RANK_AT + step)
        for at in range(0, total, block):
            stay = src[at : at + block, :]
            have = max(0, min(block, total - at - far))
            kept = jnp.where((stay & flag) != 0, 0, stay)
            if have > 0:
                move = src[at + far : at + far + have, :]
                if have < block:
                    move = jnp.concatenate(
                        [move, jnp.zeros((block - have, LANES), jnp.int32)], axis=0
                    )
                kept = jnp.where((move & flag) != 0, move, kept)
            dst[at : at + block, :] = kept
        src, dst = dst, src

    lane_row = lax.broadcasted_iota(jnp.int32, (LANES, LANES), 1)
    key_row = jnp.broadcast_to(count * LANES, (LANES, LANES)) + lane_row
    key_col = key_row.astype(F32).T
    ahead = jnp.where(key_row.astype(F32) > key_col, 1.0, 0.0)
    place = jnp.sum(ahead, axis=1, keepdims=True).astype(jnp.int32)
    order = jnp.where(place == lane_row, 1.0, 0.0).astype(BF16)

    def shuffle(values):
        got = jnp.dot(values.astype(F32).astype(BF16), order, preferred_element_type=F32)
        return got.astype(jnp.int32)

    wide = jnp.broadcast_to(count, (8, LANES))
    sorted_count = (shuffle(wide // 64) * 64 + shuffle(wide % 64))[0:1]
    lane_id = shuffle(lax.broadcasted_iota(jnp.int32, (8, LANES), 1))[0:1]
    deepest = jnp.max(count)
    fetch.wait()

    def chunk(ch, c):
        entries = src[aligned(ch, LANES), :]
        ident = (entries // 8) % (1 << 15)
        low = shuffle(ident % 256)
        high = shuffle(ident // 256)
        part = shuffle(entries % 8)
        ident = high * 256 + low
        at_row = ch * LANES + lax.broadcasted_iota(jnp.int32, (LANES, LANES), 0)
        live = sorted_count > at_row
        goal = (ident // fs) * targets + part * LANES + lane_id
        rows_v[...] = jnp.where(live, goal, nb * targets)
        front_v[...] = jnp.where(live, ident, nb * fs)
        in_row = jnp.sum(jnp.where(live, 1.0, 0.0), axis=1, keepdims=True).astype(jnp.int32)
        count_v[...] = jnp.broadcast_to((in_row + (UNROLL - 1)) // UNROLL, (LANES, LANES))
        moves = [
            pltpu.make_async_copy(rows_v, rows_s, sems.at[1]),
            pltpu.make_async_copy(front_v, front_i, sems.at[2]),
            pltpu.make_async_copy(count_v, count_s, sems.at[3]),
        ]
        for m in moves:
            m.start()
        for m in moves:
            m.wait()

        def row(r, c):
            def group(g, c):
                base = g * UNROLL
                goals = [rows_s[r, base + u] for u in range(UNROLL)]
                verts_at = [front_s[front_i[r, base + u]] for u in range(UNROLL)]
                got = [table[pl.ds(v, 1), :] for v in verts_at]
                old = [acc[pl.ds(a, 1), :] for a in goals]
                for u in range(UNROLL):
                    acc[pl.ds(goals[u], 1), :] = got[u] + old[u]
                return c

            return lax.fori_loop(0, count_s[r, 0], group, c)

        return lax.fori_loop(0, jnp.minimum(LANES, deepest - ch * LANES), row, c)

    lax.fori_loop(0, (deepest + LANES - 1) // LANES, chunk, 0)

    def mine(i, c):
        base = graph * fs + i * UNROLL
        got = [table[pl.ds(front_s[base + u], 1), :] for u in range(UNROLL)]
        for u in range(UNROLL):
            own[pl.ds(i * UNROLL + u, 1), :] = got[u]
        return c

    lax.fori_loop(0, targets // UNROLL, mine, 0)

    for b in range(nb):
        turned = [
            acc[b * targets + q * LANES : b * targets + (q + 1) * LANES, 0:width].T
            for q in range(8)
        ]
        out_ref[b] = jnp.concatenate(turned, axis=0).astype(BF16)
    turned = [own[q * LANES : (q + 1) * LANES, 0:width].T for q in range(8)]
    self_ref[...] = jnp.concatenate(turned, axis=0).astype(BF16)


def gather(feats, front, nbr, nb):
    width, verts = feats.shape
    total = nbr.shape[0]
    vmem = pl.BlockSpec(memory_space=pltpu.VMEM)
    return pl.pallas_call(
        functools.partial(gather_kernel, nb),
        out_shape=(
            jax.ShapeDtypeStruct((nb, 8 * width, LANES), BF16),
            jax.ShapeDtypeStruct((8 * width, LANES), BF16),
        ),
        in_specs=[vmem, pl.BlockSpec(memory_space=pl.ANY), vmem],
        out_specs=(vmem, vmem),
        scratch_shapes=[
            pltpu.VMEM((verts + 8, LANES), F32),
            pltpu.VMEM((nb * 8 * LANES + 8, LANES), F32),
            pltpu.VMEM((8 * LANES, LANES), F32),
            pltpu.VMEM((total + 64, LANES), jnp.int32),
            pltpu.VMEM((total + 64, LANES), jnp.int32),
            pltpu.VMEM((LANES, LANES), jnp.int32),
            pltpu.VMEM((LANES, LANES), jnp.int32),
            pltpu.VMEM((LANES, LANES), jnp.int32),
            pltpu.SMEM(front.shape, jnp.int32),
            pltpu.SMEM((LANES, LANES), jnp.int32),
            pltpu.SMEM((LANES, LANES), jnp.int32),
            pltpu.SMEM((LANES, LANES), jnp.int32),
            pltpu.SemaphoreType.DMA((4,)),
        ],
        compiler_params=pltpu.CompilerParams(vmem_limit_bytes=40 * 1024 * 1024),
        cost_estimate=pl.CostEstimate(flops=200000000, bytes_accessed=100000000, transcendentals=0),
        name="neighbour_sums",
    )(feats, front, nbr)


def split_dot(ones, wide, dims):
    high = wide.astype(BF16)
    low = (wide - high.astype(F32)).astype(BF16)
    return lax.dot_general(ones, high, dims, preferred_element_type=F32) + lax.dot_general(
        ones, low, dims, preferred_element_type=F32
    )


NN = (((1,), (0,)), ((), ()))
TN = (((0,), (0,)), ((), ()))


def layers_kernel(
    nz, ny,
    part_ref, self_ref, deg_ref, w_ref, b1_ref, w2s_ref, w2n_ref, b2_ref, dl_ref, nbr2_ref,
    logits_ref, grads_ref,
    got1, xs, got2, pre, got3, lp, got4, l2, got5, gp, gotg, gg, gotz, fy,
    s1, r1, s2, r2, s3, r3, s4, r4, s5, r5, sg, rg, sz, rz, sy, ry, sx, rx,
):
    feat = lax.axis_index("feat")
    graph = lax.axis_index("graph")
    ng = part_ref.shape[0]
    z = feat // ny
    y = feat % ny
    width = part_ref.shape[1] // 8
    cdim = w2s_ref.shape[2]

    def at_graph(d):
        return (feat, (graph + d) % ng)

    def at_z(d):
        return (((z + d) % nz) * ny + y, graph)

    def at_y(d):
        return (z * ny + (y + d) % ny, graph)

    barrier = pltpu.get_barrier_semaphore()
    for d in range(1, ng):
        pl.semaphore_signal(barrier, inc=1, device_id=at_graph(d), device_id_type=MESH)
    for d in range(1, nz):
        pl.semaphore_signal(barrier, inc=1, device_id=at_z(d), device_id_type=MESH)
    for d in range(1, ny):
        pl.semaphore_signal(barrier, inc=1, device_id=at_y(d), device_id_type=MESH)
    pl.semaphore_wait(barrier, (ng - 1) + (nz - 1) + (ny - 1))

    def send(src, dst, ssem, rsem, where):
        copy = pltpu.make_async_remote_copy(
            src_ref=src, dst_ref=dst, send_sem=ssem, recv_sem=rsem,
            device_id=where, device_id_type=MESH,
        )
        copy.start()
        return copy

    c1 = [
        send(part_ref.at[(graph + d) % ng], got1.at[d], s1.at[d], r1.at[d], at_graph(d))
        for d in range(1, ng)
    ]

    seeds = dl_ref.shape[0]
    second = nbr2_ref[...]
    deg2 = jnp.sum(jnp.where(second >= 0, 1.0, 0.0), axis=1, keepdims=True)
    spot = z * LANES + lax.broadcasted_iota(jnp.int32, (seeds, LANES), 1)
    hits = jnp.zeros((seeds, LANES), F32)
    for k in range(second.shape[1]):
        hits = hits + jnp.where(second[:, k : k + 1] == spot, 1.0, 0.0)
    hits = hits.astype(BF16)
    row = lax.broadcasted_iota(jnp.int32, (seeds, LANES), 0)
    same = jnp.where(row == spot, 1.0, 0.0).astype(BF16)
    dl = dl_ref[...]

    def exact(ones, wide):
        top = wide.astype(BF16)
        return (
            split_dot(ones, wide - top.astype(F32), TN)
            + lax.dot_general(ones, top, TN, preferred_element_type=F32)
        )

    cot = jnp.concatenate([exact(same, dl), exact(hits, dl / deg2)], axis=1)

    for c in c1:
        c.wait_recv()
    summed = part_ref[graph].astype(F32)
    for d in range(1, ng):
        summed = summed + got1[d].astype(F32)
    for q in range(8):
        xs[q, 0:width, :] = summed[q * width : (q + 1) * width] / deg_ref[q : q + 1, :]
        xs[q, width : 2 * width, :] = self_ref[q * width : (q + 1) * width, :].astype(F32)
    c2 = [
        send(xs.at[(z + d) % nz], got2.at[z], s2.at[d], r2.at[d], at_z(d)) for d in range(1, nz)
    ]
    got2[z] = xs[z]
    for c in c2:
        c.wait_recv()
    x = got2[...].reshape(nz * 2 * width, LANES)
    w = w_ref[...]
    high = x.astype(BF16)
    low = (x - high.astype(F32)).astype(BF16)
    part = lax.dot_general(high, w, TN, preferred_element_type=F32) + lax.dot_general(
        low, w, TN, preferred_element_type=F32
    )
    for k in range(ny):
        pre[k] = part[:, k * LANES : (k + 1) * LANES]
    c3 = [
        send(pre.at[(y + d) % ny], got3.at[d], s3.at[d], r3.at[d], at_y(d)) for d in range(1, ny)
    ]
    for c in c3:
        c.wait_recv()
    h = pre[y]
    for d in range(1, ny):
        h = h + got3[d]
    h = jnp.maximum(h + b1_ref[y], 0.0).astype(BF16)

    g = split_dot(h, cot, TN)
    for k in range(ng):
        gp[k] = g[k * 16 : (k + 1) * 16, :]
    cg = [
        send(gp.at[(graph + d) % ng], gotg.at[d], sg.at[d], rg.at[d], at_graph(d))
        for d in range(1, ng)
    ]

    zs = jnp.dot(h, w2s_ref[y], preferred_element_type=F32)
    zn = jnp.dot(h, w2n_ref[y], preferred_element_type=F32)
    scores = split_dot(hits, zn, NN) / deg2 + split_dot(same, zs, NN)
    for a in range(nz):
        for k in range(ny):
            base = (a * ny + k) * 8
            lp[k, a] = scores[base : base + 8, :]
    c4 = [
        send(lp.at[(y + d) % ny], got4.at[d], s4.at[d], r4.at[d], at_y(d)) for d in range(1, ny)
    ]

    for c in cg:
        c.wait_recv()
    gsum = gp[graph]
    for d in range(1, ng):
        gsum = gsum + gotg[d]
    gg[...] = gsum
    cz = [send(gg, gotz.at[z], sz.at[d], rz.at[d], at_z(d)) for d in range(1, nz)]
    gotz[z] = gsum

    for c in c4:
        c.wait_recv()
    lsum = lp[y]
    for d in range(1, ny):
        lsum = lsum + got4[d]
    l2[...] = lsum
    c5 = [
        send(l2.at[(z + d) % nz], got5.at[d], s5.at[d], r5.at[d], at_z(d)) for d in range(1, nz)
    ]

    for c in cz:
        c.wait_recv()
    whole = gotz[0]
    for k in range(1, nz):
        whole = whole + gotz[k]
    fy[y] = whole.astype(BF16)
    cy = [send(fy.at[y], fy.at[y], sy.at[d], ry.at[d], at_y(d)) for d in range(1, ny)]
    for c in cy:
        c.wait_recv()
    cx = [
        send(fy, grads_ref.at[graph], sx.at[d], rx.at[d], at_graph(d)) for d in range(1, ng)
    ]
    grads_ref[graph] = fy[...]

    for c in c5:
        c.wait_recv()
    final = l2[z] + b2_ref[...]
    for d in range(1, nz):
        final = final + got5[d]
    logits_ref[...] = final

    for c in cx:
        c.wait_recv()
    for c in c1 + c2 + c3 + cg + c4 + cz + c5 + cy + cx:
        c.wait_send()


def layers(nz, ny, part, own, deg, w, b1, w2s, w2n, b2, dl, nbr2):
    ng, rows, _ = part.shape
    width = rows // 8
    cdim = w2s.shape[2]
    vmem = pl.BlockSpec(memory_space=pltpu.VMEM)
    dma = lambda n: pltpu.SemaphoreType.DMA((n,))
    return pl.pallas_call(
        functools.partial(layers_kernel, nz, ny),
        out_shape=(
            jax.ShapeDtypeStruct((8, cdim), F32),
            jax.ShapeDtypeStruct((ng, ny, 16, 2 * cdim), BF16),
        ),
        in_specs=[vmem] * 10,
        out_specs=(vmem, vmem),
        scratch_shapes=[
            pltpu.VMEM((ng, rows, LANES), BF16),
            pltpu.VMEM((8, 2 * width, LANES), F32),
            pltpu.VMEM((nz, 2 * width, LANES), F32),
            pltpu.VMEM((ny, LANES, LANES), F32),
            pltpu.VMEM((ny, LANES, LANES), F32),
            pltpu.VMEM((ny, nz, 8, cdim), F32),
            pltpu.VMEM((ny, nz, 8, cdim), F32),
            pltpu.VMEM((nz, 8, cdim), F32),
            pltpu.VMEM((nz, 8, cdim), F32),
            pltpu.VMEM((ng, 16, 2 * cdim), F32),
            pltpu.VMEM((ng, 16, 2 * cdim), F32),
            pltpu.VMEM((16, 2 * cdim), F32),
            pltpu.VMEM((nz, 16, 2 * cdim), F32),
            pltpu.VMEM((ny, 16, 2 * cdim), BF16),
            dma(ng), dma(ng), dma(nz), dma(nz), dma(ny), dma(ny), dma(ny), dma(ny),
            dma(nz), dma(nz), dma(ng), dma(ng), dma(nz), dma(nz), dma(ny), dma(ny),
            dma(ng), dma(ng),
        ],
        compiler_params=pltpu.CompilerParams(
            collective_id=0, has_side_effects=True, vmem_limit_bytes=40 * 1024 * 1024
        ),
        cost_estimate=pl.CostEstimate(flops=300000000, bytes_accessed=10000000, transcendentals=0),
        name="layers",
    )(part, own, deg, w, b1, w2s, w2n, b2, dl, nbr2)


def on_device(feats, front_ids, nbr1, nbr2, w1_self, w1_neigh, b1, w2_self, w2_neigh, b2, dlogits):
    owner = lax.axis_index("graph")
    nb, targets, fan = nbr1.shape
    width, verts = feats.shape
    hidden, cdim = w2_self.shape
    nz, ny = 8, 4

    groups = [[a * ny + k for a in range(nz)] for k in range(ny)]
    w = lax.all_gather(
        jnp.concatenate([w1_neigh, w1_self], axis=0), "feat",
        axis_index_groups=groups, axis=0, tiled=True,
    )
    side = jnp.concatenate([dlogits[0], nbr2[0].astype(F32)], axis=1)
    side = lax.all_gather(side, "feat", axis=0, tiled=True)
    dl = side[:, :cdim]
    second = side[:, cdim:].astype(jnp.int32)

    front = front_ids[:, 0, :].reshape(-1)
    front = jnp.concatenate([front, jnp.full((FRONT_PAD,), verts, jnp.int32)])
    turned = nbr1.transpose(0, 2, 1)
    own_deg = lax.dynamic_index_in_dim(turned, owner, 0, keepdims=False)
    deg = jnp.sum(own_deg >= 0, axis=0).astype(F32).reshape(8, LANES)
    part, own = gather(feats, front, turned.reshape(nb * fan * 8, LANES), nb)

    b1y = b1.reshape(ny, 1, LANES)
    w2s = w2_self.reshape(ny, LANES, cdim)
    w2n = w2_neigh.reshape(ny, LANES, cdim)
    logits, grads = layers(
        nz, ny, part, own, deg, w, b1y, w2s, w2n, b2.reshape(1, cdim), dl, second
    )
    grads = grads.transpose(1, 0, 2, 3).reshape(hidden, 2 * cdim).astype(F32)
    return (logits[None], grads[:, :cdim], grads[:, cdim:])


def solution(mesh):
    in_specs = (
        P("feat", "graph"),
        P(None, "graph", None),
        P(),
        P("graph", "feat", None),
        P("feat", None),
        P("feat", None),
        P(),
        P(),
        P(),
        P(),
        P("graph", "feat", None),
    )
    out_specs = (P("graph", "feat", None), P(), P())
    return jax.shard_map(
        on_device, mesh=mesh, in_specs=in_specs, out_specs=out_specs, check_vma=False
    )
```

```python
import functools

import jax
import jax.numpy as jnp
from jax import lax
from jax.experimental import pallas as pl
from jax.experimental.pallas import tpu as pltpu
from jax.sharding import PartitionSpec as P

LANES = 128
UNROLL = 8
CHUNK = 32
FRONT_PAD = 1024
WORD_BITS = 16
WORD = 1 << WORD_BITS
MESH = pl.DeviceIdType.MESH
F32 = jnp.float32
BF16 = jnp.bfloat16
VALID = 1 << 29
RANK_AT = 18


def aligned(index, size):
    return pl.ds(pl.multiple_of(index * size, size), size)


def gather_kernel(
    nb, feats_ref, front_ref, nbr_ref, out_ref, self_ref, deg_ref,
    table, acc, own, one, two, lists_v, lists_s, front_s, sems, front_sem,
):
    width = feats_ref.shape[0]
    verts = feats_ref.shape[1]
    total = nbr_ref.shape[0]
    per = total // nb
    targets = 8 * LANES
    fs = (front_ref.shape[0] - FRONT_PAD) // nb
    fs_bits = fs.bit_length() - 1
    graph = lax.axis_index("graph")

    fetch = pltpu.make_async_copy(front_ref, front_s, front_sem)
    fetch.start()

    def turn(i, c):
        block = feats_ref[:, aligned(i, LANES)].astype(F32)
        table[aligned(i, LANES), 0:width] = block.T
        return c

    lax.fori_loop(0, verts // LANES, turn, 0, unroll=4)
    table[verts : verts + 8, :] = jnp.zeros((8, LANES), F32)

    def clear(i, c):
        acc[aligned(i, 64), :] = jnp.zeros((64, LANES), F32)
        return c

    lax.fori_loop(0, nb * targets // 64, clear, 0, unroll=4)
    acc[nb * targets : nb * targets + 8, :] = jnp.zeros((8, LANES), F32)

    degree = jnp.zeros((8, LANES), F32)
    for k in range(per // 8):
        ids = nbr_ref[pl.ds(pl.multiple_of(graph * per + k * 8, 8), 8), :]
        degree = degree + jnp.where(ids >= 0, 1.0, 0.0)
    deg_ref[...] = degree

    below = (
        lax.broadcasted_iota(jnp.int32, (per, per), 0)
        > lax.broadcasted_iota(jnp.int32, (per, per), 1)
    ).astype(F32).astype(BF16)
    sub = lax.broadcasted_iota(jnp.int32, (per, LANES), 0) % 8
    lost = jnp.zeros((1, LANES), jnp.int32)
    for b in range(nb):
        ids = nbr_ref[b * per : (b + 1) * per, :]
        here = (ids >> fs_bits) == graph
        gone = jnp.where(here, 0.0, 1.0)
        before = jnp.dot(below, gone.astype(BF16), preferred_element_type=F32)
        rank = before.astype(jnp.int32) + lost
        entry = VALID + rank * (1 << RANK_AT) + ((ids & (fs - 1)) + b * fs) * 8 + sub
        one[b * per : (b + 1) * per, :] = jnp.where(here, entry, 0)
        lost = lost + jnp.sum(gone, axis=0, keepdims=True).astype(jnp.int32)
    count = total - lost

    src, dst = one, two
    bits = (total - 1).bit_length()
    block = 64
    for step in range(bits):
        far = 1 << step
        flag = 1 << (RANK_AT + step)
        for at in range(0, total, block):
            stay = src[at : at + block, :]
            have = max(0, min(block, total - at - far))
            kept = jnp.where((stay & flag) != 0, 0, stay)
            if have > 0:
                move = src[at + far : at + far + have, :]
                if have < block:
                    move = jnp.concatenate(
                        [move, jnp.zeros((block - have, LANES), jnp.int32)], axis=0
                    )
                kept = jnp.where((move & flag) != 0, move, kept)
            dst[at : at + block, :] = kept
        src, dst = dst, src

    lane_row = lax.broadcasted_iota(jnp.int32, (LANES, LANES), 1)
    key_row = jnp.broadcast_to(count * LANES, (LANES, LANES)) + lane_row
    key_col = key_row.astype(F32).T
    ahead = jnp.where(key_row.astype(F32) > key_col, 1.0, 0.0)
    place = jnp.sum(ahead, axis=1, keepdims=True).astype(jnp.int32)
    order = jnp.where(place == lane_row, 1.0, 0.0).astype(BF16)

    def shuffle(values):
        got = jnp.dot(values.astype(F32).astype(BF16), order, preferred_element_type=F32)
        return got.astype(jnp.int32)

    wide = jnp.broadcast_to(count, (8, LANES))
    sorted_count = (shuffle(wide // 64) * 64 + shuffle(wide % 64))[0:1]
    lane_id = shuffle(lax.broadcasted_iota(jnp.int32, (8, LANES), 1))[0:1]
    count_col = jnp.broadcast_to(sorted_count.astype(F32), (LANES, LANES)).T
    deepest = jnp.max(count)
    chunks = (deepest + CHUNK - 1) // CHUNK

    def prepare(ch, slot):
        entries = src[aligned(ch, CHUNK), :]
        ident = (entries >> 3) & (nb * fs - 1)
        ident = shuffle(ident >> 8) * 256 + shuffle(ident & 255)
        group = shuffle(entries & 7)
        at_row = ch * CHUNK + lax.broadcasted_iota(jnp.int32, (CHUNK, LANES), 0)
        live = sorted_count > at_row
        goal = (ident >> fs_bits) * targets + group * LANES + lane_id
        word = jnp.where(live, goal * WORD + ident, nb * targets * WORD + nb * fs)
        lists_v[slot, 0:CHUNK, :] = word
        row_at = (ch * CHUNK + lane_row).astype(F32)
        in_row = jnp.sum(jnp.where(count_col > row_at, 1.0, 0.0), axis=0, keepdims=True)
        groups = (in_row.astype(jnp.int32) + (UNROLL - 1)) // UNROLL
        lists_v[slot, CHUNK : CHUNK + 8, :] = jnp.broadcast_to(groups, (8, LANES))

    def transfer(slot):
        return pltpu.make_async_copy(
            lists_v.at[slot],
            lists_s.at[pl.ds(pl.multiple_of(slot * (CHUNK + 8), 8), CHUNK + 8)],
            sems.at[slot],
        )

    @pl.when(chunks > 0)
    def _():
        prepare(0, 0)
        transfer(0).start()

    fetch.wait()

    def chunk(ch, c):
        slot = ch & 1
        base = slot * (CHUNK + 8)
        transfer(slot).wait()

        @pl.when(ch + 1 < chunks)
        def _():
            prepare(ch + 1, 1 - slot)
            transfer(1 - slot).start()

        def row(r, c):
            def group(g):
                words = [lists_s[at, g * UNROLL + u] for u in range(UNROLL)]
                got = [table[pl.ds(front_s[w & (WORD - 1)], 1), :] for w in words]
                goals = [w >> WORD_BITS for w in words]
                old = [acc[pl.ds(a, 1), :] for a in goals]
                for u in range(UNROLL):
                    acc[pl.ds(goals[u], 1), :] = got[u] + old[u]

            groups = lists_s[base + CHUNK, r]
            at = base + r
            every = LANES // UNROLL

            @pl.when(groups == every)
            def _():
                for g in range(every):
                    group(g)

            @pl.when(groups < every)
            def _():
                for g in range(every):
                    pl.when(g < groups)(functools.partial(group, g))

            return c

        return lax.fori_loop(0, jnp.minimum(CHUNK, deepest - ch * CHUNK), row, c)

    lax.fori_loop(0, chunks, chunk, 0)

    def mine(i, c):
        base = graph * fs + i * UNROLL
        got = [table[pl.ds(front_s[base + u], 1), :] for u in range(UNROLL)]
        for u in range(UNROLL):
            own[pl.ds(i * UNROLL + u, 1), :] = got[u]
        return c

    lax.fori_loop(0, targets // UNROLL, mine, 0)

    for b in range(nb):
        turned = [
            acc[b * targets + q * LANES : b * targets + (q + 1) * LANES, 0:width].T
            for q in range(8)
        ]
        out_ref[b] = jnp.concatenate(turned, axis=0).astype(BF16)
    turned = [own[q * LANES : (q + 1) * LANES, 0:width].T for q in range(8)]
    self_ref[...] = jnp.concatenate(turned, axis=0).astype(BF16)


def gather(feats, front, nbr, nb):
    width, verts = feats.shape
    total = nbr.shape[0]
    vmem = pl.BlockSpec(memory_space=pltpu.VMEM)
    return pl.pallas_call(
        functools.partial(gather_kernel, nb),
        out_shape=(
            jax.ShapeDtypeStruct((nb, 8 * width, LANES), BF16),
            jax.ShapeDtypeStruct((8 * width, LANES), BF16),
            jax.ShapeDtypeStruct((8, LANES), F32),
        ),
        in_specs=[vmem, pl.BlockSpec(memory_space=pl.ANY), vmem],
        out_specs=(vmem, vmem, vmem),
        scratch_shapes=[
            pltpu.VMEM((verts + 8, LANES), F32),
            pltpu.VMEM((nb * 8 * LANES + 8, LANES), F32),
            pltpu.VMEM((8 * LANES, LANES), F32),
            pltpu.VMEM((total + 64, LANES), jnp.int32),
            pltpu.VMEM((total + 64, LANES), jnp.int32),
            pltpu.VMEM((2, CHUNK + 8, LANES), jnp.int32),
            pltpu.SMEM((2 * (CHUNK + 8), LANES), jnp.int32),
            pltpu.SMEM(front.shape, jnp.int32),
            pltpu.SemaphoreType.DMA((2,)),
            pltpu.SemaphoreType.DMA,
        ],
        compiler_params=pltpu.CompilerParams(vmem_limit_bytes=40 * 1024 * 1024),
        cost_estimate=pl.CostEstimate(flops=200000000, bytes_accessed=100000000, transcendentals=0),
        name="neighbour_sums",
    )(feats, front, nbr)


def split_dot(ones, wide, dims):
    high = wide.astype(BF16)
    low = (wide - high.astype(F32)).astype(BF16)
    return lax.dot_general(ones, high, dims, preferred_element_type=F32) + lax.dot_general(
        ones, low, dims, preferred_element_type=F32
    )


NN = (((1,), (0,)), ((), ()))
TN = (((0,), (0,)), ((), ()))


def layers_kernel(
    nz, ny,
    part_ref, self_ref, deg_ref, w_ref, b1_ref, w2s_ref, w2n_ref, b2_ref, side_ref,
    logits_ref, grads_ref,
    gotw, sv, sall, got1, xs, got2, pre, got3, lp, got4, l2, got5, gp, gotg, gg, gotz, fy,
    sw, rw, sf, rf, sa, ra, sb, rb, s1, r1, s2, r2, s3, r3, s4, r4, s5, r5, sg, rg, sz, rz, sy, ry, sx, rx,
):
    feat = lax.axis_index("feat")
    graph = lax.axis_index("graph")
    ng = part_ref.shape[0]
    z = feat // ny
    y = feat % ny
    width = part_ref.shape[1] // 8
    cdim = w2s_ref.shape[2]

    def at_graph(d):
        return (feat, (graph + d) % ng)

    def at_z(d):
        return (((z + d) % nz) * ny + y, graph)

    def at_y(d):
        return (z * ny + (y + d) % ny, graph)

    barrier = pltpu.get_barrier_semaphore()
    for d in range(1, ng):
        pl.semaphore_signal(barrier, inc=1, device_id=at_graph(d), device_id_type=MESH)
    for d in range(1, nz):
        pl.semaphore_signal(barrier, inc=1, device_id=at_z(d), device_id_type=MESH)
    for d in range(1, ny):
        pl.semaphore_signal(barrier, inc=1, device_id=at_y(d), device_id_type=MESH)
    pl.semaphore_wait(barrier, (ng - 1) + (nz - 1) + (ny - 1))

    def send(src, dst, ssem, rsem, where):
        copy = pltpu.make_async_remote_copy(
            src_ref=src, dst_ref=dst, send_sem=ssem, recv_sem=rsem,
            device_id=where, device_id_type=MESH,
        )
        copy.start()
        return copy

    c1 = [
        send(part_ref.at[(graph + d) % ng], got1.at[d], s1.at[d], r1.at[d], at_graph(d))
        for d in range(1, ng)
    ]

    ca = [send(side_ref, sv.at[z], sa.at[d], ra.at[d], at_z(d)) for d in range(1, nz)]
    sv[z] = side_ref[...]

    core = graph % 2
    sibling = (feat, graph + 1 - 2 * core)

    def weight_copy(d):
        return pltpu.make_async_remote_copy(
            src_ref=w_ref, dst_ref=gotw.at[z], send_sem=sw.at[d], recv_sem=rw.at[d],
            device_id=at_z(d), device_id_type=MESH,
        )

    def weight_pass(d):
        block = gotw.at[(z - d + nz) % nz]
        return pltpu.make_async_remote_copy(
            src_ref=block, dst_ref=block, send_sem=sf.at[d], recv_sem=rf.at[d],
            device_id=sibling, device_id_type=MESH,
        )

    @pl.when(z % 2 == core)
    def _():
        for d in range(1, nz):
            weight_copy(d).start()

    gotw[z] = w_ref[...]

    for c in ca:
        c.wait_recv()
    cb = [send(sv, sall.at[y], sb.at[d], rb.at[d], at_y(d)) for d in range(1, ny)]
    sall[y] = sv[...]

    for d in range(1, nz):
        @pl.when((z + d) % 2 == core)
        def _():
            weight_copy(d).wait_recv()
            weight_pass(d).start()

    for c in cb:
        c.wait_recv()

    side = sall[...].reshape(ny * nz * 8, side_ref.shape[1])
    seeds = ny * nz * 8
    dl = side[:, :cdim]
    second = side[:, cdim:].astype(jnp.int32)
    deg2 = jnp.sum(jnp.where(second >= 0, 1.0, 0.0), axis=1, keepdims=True)
    spot = z * LANES + lax.broadcasted_iota(jnp.int32, (seeds, LANES), 1)
    hits = jnp.zeros((seeds, LANES), F32)
    for k in range(second.shape[1]):
        hits = hits + jnp.where(second[:, k : k + 1] == spot, 1.0, 0.0)
    hits = hits.astype(BF16)
    at = lax.broadcasted_iota(jnp.int32, (seeds, LANES), 0)
    row = ((at // 8) % nz) * (ny * 8) + (at // (8 * nz)) * 8 + at % 8
    same = jnp.where(row == spot, 1.0, 0.0).astype(BF16)

    def exact(ones, wide):
        top = wide.astype(BF16)
        return (
            split_dot(ones, wide - top.astype(F32), TN)
            + lax.dot_general(ones, top, TN, preferred_element_type=F32)
        )

    cot = jnp.concatenate([exact(same, dl), exact(hits, dl / deg2)], axis=1)

    for c in c1:
        c.wait_recv()
    summed = part_ref[graph].astype(F32)
    for d in range(1, ng):
        summed = summed + got1[d].astype(F32)
    for q in range(8):
        xs[q, 0:width, :] = summed[q * width : (q + 1) * width] / deg_ref[q : q + 1, :]
        xs[q, width : 2 * width, :] = self_ref[q * width : (q + 1) * width, :].astype(F32)
    c2 = [
        send(xs.at[(z + d) % nz], got2.at[z], s2.at[d], r2.at[d], at_z(d)) for d in range(1, nz)
    ]
    got2[z] = xs[z]
    for c in c2:
        c.wait_recv()
    x = got2[...].reshape(nz * 2 * width, LANES)
    for d in range(1, nz):
        @pl.when((z + d) % 2 != core)
        def _():
            weight_pass(d).wait_recv()
    w = gotw[...].reshape(nz * 2 * width, w_ref.shape[1])
    high = x.astype(BF16)
    low = (x - high.astype(F32)).astype(BF16)
    part = lax.dot_general(high, w, TN, preferred_element_type=F32) + lax.dot_general(
        low, w, TN, preferred_element_type=F32
    )
    for k in range(ny):
        pre[k] = part[:, k * LANES : (k + 1) * LANES]
    c3 = [
        send(pre.at[(y + d) % ny], got3.at[d], s3.at[d], r3.at[d], at_y(d)) for d in range(1, ny)
    ]
    for c in c3:
        c.wait_recv()
    h = pre[y]
    for d in range(1, ny):
        h = h + got3[d]
    h = jnp.maximum(h + b1_ref[y], 0.0).astype(BF16)

    g = split_dot(h, cot, TN)
    for k in range(ng):
        gp[k] = g[k * 16 : (k + 1) * 16, :]
    cg = [
        send(gp.at[(graph + d) % ng], gotg.at[d], sg.at[d], rg.at[d], at_graph(d))
        for d in range(1, ng)
    ]

    zs = jnp.dot(h, w2s_ref[y], preferred_element_type=F32)
    zn = jnp.dot(h, w2n_ref[y], preferred_element_type=F32)
    scores = split_dot(hits, zn, NN) / deg2 + split_dot(same, zs, NN)
    lp[...] = scores.reshape(ny, nz, 8, cdim)
    c4 = [
        send(lp.at[(y + d) % ny], got4.at[d], s4.at[d], r4.at[d], at_y(d)) for d in range(1, ny)
    ]

    for c in cg:
        c.wait_recv()
    gsum = gp[graph]
    for d in range(1, ng):
        gsum = gsum + gotg[d]
    gg[...] = gsum
    cz = [send(gg, gotz.at[z], sz.at[d], rz.at[d], at_z(d)) for d in range(1, nz)]
    gotz[z] = gsum

    for c in c4:
        c.wait_recv()
    lsum = lp[y]
    for d in range(1, ny):
        lsum = lsum + got4[d]
    l2[...] = lsum
    c5 = [
        send(l2.at[(z + d) % nz], got5.at[d], s5.at[d], r5.at[d], at_z(d)) for d in range(1, nz)
    ]

    for c in cz:
        c.wait_recv()
    whole = gotz[0]
    for k in range(1, nz):
        whole = whole + gotz[k]
    fy[y] = whole.astype(BF16)
    cy = [send(fy.at[y], fy.at[y], sy.at[d], ry.at[d], at_y(d)) for d in range(1, ny)]
    for c in cy:
        c.wait_recv()
    cx = [
        send(fy, grads_ref.at[graph], sx.at[d], rx.at[d], at_graph(d)) for d in range(1, ng)
    ]
    grads_ref[graph] = fy[...]

    for c in c5:
        c.wait_recv()
    final = l2[z] + b2_ref[...]
    for d in range(1, nz):
        final = final + got5[d]
    logits_ref[...] = final

    for c in cx:
        c.wait_recv()
    for c in ca + cb + c1 + c2 + c3 + cg + c4 + cz + c5 + cy + cx:
        c.wait_send()

    @pl.when(z % 2 == core)
    def _():
        for d in range(1, nz):
            weight_copy(d).wait_send()

    for d in range(1, nz):
        @pl.when((z + d) % 2 == core)
        def _():
            weight_pass(d).wait_send()


def layers(nz, ny, part, own, deg, w, b1, w2s, w2n, b2, side):
    ng, rows, _ = part.shape
    width = rows // 8
    cdim = w2s.shape[2]
    vmem = pl.BlockSpec(memory_space=pltpu.VMEM)
    dma = lambda n: pltpu.SemaphoreType.DMA((n,))
    return pl.pallas_call(
        functools.partial(layers_kernel, nz, ny),
        out_shape=(
            jax.ShapeDtypeStruct((8, cdim), F32),
            jax.ShapeDtypeStruct((ng, ny, 16, 2 * cdim), BF16),
        ),
        in_specs=[vmem] * 9,
        out_specs=(vmem, vmem),
        scratch_shapes=[
            pltpu.VMEM((nz, 2 * width, w.shape[1]), BF16),
            pltpu.VMEM((nz,) + side.shape, F32),
            pltpu.VMEM((ny, nz) + side.shape, F32),
            pltpu.VMEM((ng, rows, LANES), BF16),
            pltpu.VMEM((8, 2 * width, LANES), F32),
            pltpu.VMEM((nz, 2 * width, LANES), F32),
            pltpu.VMEM((ny, LANES, LANES), F32),
            pltpu.VMEM((ny, LANES, LANES), F32),
            pltpu.VMEM((ny, nz, 8, cdim), F32),
            pltpu.VMEM((ny, nz, 8, cdim), F32),
            pltpu.VMEM((nz, 8, cdim), F32),
            pltpu.VMEM((nz, 8, cdim), F32),
            pltpu.VMEM((ng, 16, 2 * cdim), F32),
            pltpu.VMEM((ng, 16, 2 * cdim), F32),
            pltpu.VMEM((16, 2 * cdim), F32),
            pltpu.VMEM((nz, 16, 2 * cdim), F32),
            pltpu.VMEM((ny, 16, 2 * cdim), BF16),
            dma(nz), dma(nz), dma(nz), dma(nz), dma(nz), dma(nz), dma(ny), dma(ny),
            dma(ng), dma(ng), dma(nz), dma(nz), dma(ny), dma(ny), dma(ny), dma(ny),
            dma(nz), dma(nz), dma(ng), dma(ng), dma(nz), dma(nz), dma(ny), dma(ny),
            dma(ng), dma(ng),
        ],
        compiler_params=pltpu.CompilerParams(
            collective_id=0, has_side_effects=True, vmem_limit_bytes=40 * 1024 * 1024
        ),
        cost_estimate=pl.CostEstimate(flops=300000000, bytes_accessed=10000000, transcendentals=0),
        name="layers",
    )(part, own, deg, w, b1, w2s, w2n, b2, side)


def on_device(feats, front_ids, nbr1, nbr2, w1_self, w1_neigh, b1, w2_self, w2_neigh, b2, dlogits):
    nb, targets, fan = nbr1.shape
    width, verts = feats.shape
    hidden, cdim = w2_self.shape
    nz, ny = 8, 4

    w = jnp.concatenate([w1_neigh, w1_self], axis=0)
    side = jnp.concatenate([dlogits[0], nbr2[0].astype(F32)], axis=1)

    front = front_ids.reshape(-1)
    front = jnp.concatenate([front, jnp.full((FRONT_PAD,), verts, jnp.int32)])
    turned = nbr1.transpose(0, 2, 1)
    part, own, deg = gather(feats, front, turned.reshape(nb * fan * 8, LANES), nb)

    b1y = b1.reshape(ny, 1, LANES)
    w2s = w2_self.reshape(ny, LANES, cdim)
    w2n = w2_neigh.reshape(ny, LANES, cdim)
    logits, grads = layers(
        nz, ny, part, own, deg, w, b1y, w2s, w2n, b2.reshape(1, cdim), side
    )
    grads = grads.transpose(1, 0, 2, 3).reshape(hidden, 2 * cdim).astype(F32)
    return (logits[None], grads[:, :cdim], grads[:, cdim:])


def solution(mesh):
    in_specs = (
        P("feat", "graph"),
        P(None, "graph", None),
        P(),
        P("graph", "feat", None),
        P("feat", None),
        P("feat", None),
        P(),
        P(),
        P(),
        P(),
        P("graph", "feat", None),
    )
    out_specs = (P("graph", "feat", None), P(), P())
    return jax.shard_map(
        on_device, mesh=mesh, in_specs=in_specs, out_specs=out_specs, check_vma=False
    )
```

```python
import functools

import jax
import jax.numpy as jnp
from jax import lax
from jax.experimental import pallas as pl
from jax.experimental.pallas import tpu as pltpu
from jax.sharding import PartitionSpec as P

LANES = 128
UNROLL = 4
BLOCK = 8
CHUNK = 32
CLASSES = 160
FAN2 = 15
DENSE = 8
WORD_BITS = 15
WORD = 1 << WORD_BITS
MESH = pl.DeviceIdType.MESH
F32 = jnp.float32
BF16 = jnp.bfloat16
VALID = 1 << 29
RANK_AT = 18


def aligned(index, size):
    return pl.ds(pl.multiple_of(index * size, size), size)


def gather_kernel(
    nb, feats_ref, front_ref, ids_ref, nbr_ref, wn_ref, ws_ref, dl_ref, second_ref,
    out_ref, self_ref, deg_ref, w_ref, side_ref,
    table, acc, own, one, two, pairs_v, lists_v, pairs_s, lists_s, front_s, sems, front_sem, pair_sem,
):
    width = feats_ref.shape[0]
    verts = feats_ref.shape[1]
    fan = nbr_ref.shape[0]
    per = fan * nb
    total = per * 8
    targets = 8 * LANES
    fs = front_ref.shape[0] // nb
    fs_bits = fs.bit_length() - 1
    graph = lax.axis_index("graph")

    fetch = pltpu.make_async_copy(front_ref, front_s, front_sem)
    fetch.start()

    def turn(i, c):
        block = feats_ref[:, aligned(i, LANES)].astype(F32)
        table[aligned(i, LANES), 0:width] = block.T
        return c

    lax.fori_loop(0, verts // LANES, turn, 0, unroll=4)
    table[verts : verts + 8, :] = jnp.zeros((8, LANES), F32)

    acc[nb * targets : nb * targets + 8, :] = jnp.zeros((8, LANES), F32)

    w_ref[...] = jnp.concatenate(
        [wn_ref[...].astype(F32), ws_ref[...].astype(F32)], axis=0
    ).astype(BF16)
    side_ref[...] = jnp.zeros_like(side_ref)
    side_ref[:, 0 : dl_ref.shape[1]] = dl_ref[...]
    side_ref[:, CLASSES : CLASSES + second_ref.shape[1]] = second_ref[...].astype(F32)
    degree = jnp.zeros((1, targets), F32)
    for k in range(fan):
        degree = degree + jnp.where(nbr_ref[k, pl.ds(graph, 1), :] >= 0, 1.0, 0.0)
    deg_ref[...] = degree

    part = (nb, targets)
    start = lax.broadcasted_iota(jnp.int32, part, 0) * fs
    tile = lax.broadcasted_iota(jnp.int32, part, 1) >> 7
    seen = jnp.zeros(part, jnp.int32)
    pair = [jnp.zeros(part, jnp.int32), jnp.zeros(part, jnp.int32)]
    for k in range(fan):
        ids = nbr_ref[k]
        here = (ids >> fs_bits) == graph
        local = ids & (fs - 1)
        for j in range(2):
            pair[j] = jnp.where(here & (seen == j), local, pair[j])
        entry = jnp.where(here & (seen > 1), VALID + (local + start) * 8 + tile, 0)
        for q in range(8):
            one[q * per + k * nb : q * per + (k + 1) * nb, :] = entry[
                :, q * LANES : (q + 1) * LANES
            ]
        seen = seen + jnp.where(here, 1, 0)
    for q in range(8):
        cut = slice(q * LANES, (q + 1) * LANES)
        found = [jnp.zeros((nb, LANES), jnp.int32), jnp.zeros((nb, LANES), jnp.int32)]
        for k in range(fs // LANES):
            line = ids_ref[:, k * LANES : (k + 1) * LANES]
            for j in range(2):
                at = pair[j][:, cut]
                got = jnp.take_along_axis(line, at & (LANES - 1), axis=1)
                found[j] = jnp.where((at >> 7) == k, got, found[j])
        for j in range(2):
            found[j] = jnp.where(seen[:, cut] > j, found[j], verts)
        pairs_v[q * nb : (q + 1) * nb, :] = found[1] * WORD + found[0]
    pairs = pltpu.make_async_copy(pairs_v, pairs_s, pair_sem)
    pairs.start()

    below = (
        lax.broadcasted_iota(jnp.int32, (per, per), 0)
        > lax.broadcasted_iota(jnp.int32, (per, per), 1)
    ).astype(F32).astype(BF16)
    lost = jnp.zeros((1, LANES), jnp.int32)
    for q in range(8):
        entry = one[q * per : (q + 1) * per, :]
        gone = jnp.where(entry == 0, 1.0, 0.0)
        before = jnp.dot(below, gone.astype(BF16), preferred_element_type=F32)
        rank = before.astype(jnp.int32) + lost
        one[q * per : (q + 1) * per, :] = jnp.where(entry == 0, 0, entry + rank * (1 << RANK_AT))
        lost = lost + jnp.sum(gone, axis=0, keepdims=True).astype(jnp.int32)
    count = total - lost

    src, dst = one, two
    bits = (total - 1).bit_length()
    block = 64
    for step in range(bits):
        far = 1 << step
        flag = 1 << (RANK_AT + step)
        for at in range(0, total, block):
            stay = src[at : at + block, :]
            have = max(0, min(block, total - at - far))
            kept = jnp.where((stay & flag) != 0, 0, stay)
            if have > 0:
                move = src[at + far : at + far + have, :]
                if have < block:
                    move = jnp.concatenate(
                        [move, jnp.zeros((block - have, LANES), jnp.int32)], axis=0
                    )
                kept = jnp.where((move & flag) != 0, move, kept)
            dst[at : at + block, :] = kept
        src, dst = dst, src

    lane_row = lax.broadcasted_iota(jnp.int32, (LANES, LANES), 1)
    key_row = jnp.broadcast_to(count * LANES, (LANES, LANES)) + lane_row
    key_col = key_row.astype(F32).T
    ahead = jnp.where(key_row.astype(F32) > key_col, 1.0, 0.0)
    place = jnp.sum(ahead, axis=1, keepdims=True).astype(jnp.int32)
    order = jnp.where(place == lane_row, 1.0, 0.0).astype(BF16)

    def shuffle(values):
        got = jnp.dot(values.astype(F32).astype(BF16), order, preferred_element_type=F32)
        return got.astype(jnp.int32)

    wide = jnp.broadcast_to(count, (8, LANES))
    sorted_count = (shuffle(wide // 64) * 64 + shuffle(wide % 64))[0:1]
    lane_id = shuffle(lax.broadcasted_iota(jnp.int32, (8, LANES), 1))[0:1]
    count_col = jnp.broadcast_to(sorted_count.astype(F32), (LANES, LANES)).T
    deepest = jnp.max(count)
    chunks = (deepest + CHUNK - 1) // CHUNK

    def prepare(ch, slot):
        entries = src[aligned(ch, CHUNK), :]
        ident = (entries >> 3) & (nb * fs - 1)
        ident = shuffle(ident >> 8) * 256 + shuffle(ident & 255)
        group = shuffle(entries & 7)
        at_row = ch * CHUNK + lax.broadcasted_iota(jnp.int32, (CHUNK, LANES), 0)
        live = sorted_count > at_row
        goal = (ident >> fs_bits) * targets + group * LANES + lane_id
        word = jnp.where(live, goal * WORD + ident, nb * targets * WORD)
        lists_v[slot, 0:CHUNK, :] = word
        row_at = (ch * CHUNK + lane_row).astype(F32)
        in_row = jnp.sum(jnp.where(count_col > row_at, 1.0, 0.0), axis=0, keepdims=True)
        groups = (in_row.astype(jnp.int32) + (UNROLL - 1)) // UNROLL
        lists_v[slot, CHUNK : CHUNK + 8, :] = jnp.broadcast_to(groups, (8, LANES))

    def transfer(slot):
        return pltpu.make_async_copy(
            lists_v.at[slot],
            lists_s.at[pl.ds(pl.multiple_of(slot * (CHUNK + 8), 8), CHUNK + 8)],
            sems.at[slot],
        )

    @pl.when(chunks > 0)
    def _():
        prepare(0, 0)
        transfer(0).start()

    fetch.wait()
    pairs.wait()

    def dense(r, c):
        base = (r & (nb - 1)) * targets + (r >> (nb.bit_length() - 1)) * LANES
        for at in range(0, LANES, DENSE):
            words = [pairs_s[r, at + u] for u in range(DENSE)]
            got = [
                table[pl.ds(w & (WORD - 1), 1), :] + table[pl.ds(w >> WORD_BITS, 1), :]
                for w in words
            ]
            for u in range(DENSE):
                acc[pl.ds(pl.multiple_of(base, LANES) + at + u, 1), :] = got[u]
        return c

    lax.fori_loop(0, nb * 8, dense, 0)

    def chunk(ch, c):
        slot = ch & 1
        base = slot * (CHUNK + 8)
        transfer(slot).wait()

        @pl.when(ch + 1 < chunks)
        def _():
            prepare(ch + 1, 1 - slot)
            transfer(1 - slot).start()

        def row(r, c):
            def group(g):
                words = [lists_s[at, g * UNROLL + u] for u in range(UNROLL)]
                got = [table[pl.ds(front_s[w & (WORD - 1)], 1), :] for w in words]
                goals = [w >> WORD_BITS for w in words]
                old = [acc[pl.ds(a, 1), :] for a in goals]
                for u in range(UNROLL):
                    acc[pl.ds(goals[u], 1), :] = got[u] + old[u]

            groups = lists_s[base + CHUNK, r]
            at = base + r

            def block(h):
                for g in range(h * BLOCK, (h + 1) * BLOCK):
                    group(g)

            for h in range(LANES // UNROLL // BLOCK):
                pl.when(h * BLOCK < groups)(functools.partial(block, h))
            return c

        return lax.fori_loop(0, jnp.minimum(CHUNK, deepest - ch * CHUNK), row, c)

    lax.fori_loop(0, chunks, chunk, 0)

    def mine(i, c):
        base = graph * fs + i * UNROLL
        got = [table[pl.ds(front_s[base + u], 1), :] for u in range(UNROLL)]
        for u in range(UNROLL):
            own[pl.ds(i * UNROLL + u, 1), :] = got[u]
        return c

    lax.fori_loop(0, targets // UNROLL, mine, 0)

    for b in range(nb):
        turned = [
            acc[b * targets + q * LANES : b * targets + (q + 1) * LANES, 0:width].T
            for q in range(8)
        ]
        out_ref[b] = jnp.concatenate(turned, axis=0).astype(BF16)
    for q in range(8):
        self_ref[q] = own[q * LANES : (q + 1) * LANES, 0:width].T


def gather(feats, front, ids, nbr, wn, ws, dl, second, nb):
    width, verts = feats.shape
    total = nbr.shape[0] * nb * 8
    vmem = pl.BlockSpec(memory_space=pltpu.VMEM)
    return pl.pallas_call(
        functools.partial(gather_kernel, nb),
        out_shape=(
            jax.ShapeDtypeStruct((nb, 8 * width, LANES), BF16),
            jax.ShapeDtypeStruct((8, width, LANES), F32),
            jax.ShapeDtypeStruct((1, 8 * LANES), F32),
            jax.ShapeDtypeStruct((2 * width, wn.shape[1]), BF16),
            jax.ShapeDtypeStruct((8, CLASSES + 16), F32),
        ),
        in_specs=[vmem, pl.BlockSpec(memory_space=pl.ANY)] + [vmem] * 6,
        out_specs=(vmem,) * 5,
        scratch_shapes=[
            pltpu.VMEM((verts + 8, LANES), F32),
            pltpu.VMEM((nb * 8 * LANES + 8, LANES), F32),
            pltpu.VMEM((8 * LANES, LANES), F32),
            pltpu.VMEM((total + 64, LANES), jnp.int32),
            pltpu.VMEM((total + 64, LANES), jnp.int32),
            pltpu.VMEM((nb * 8, LANES), jnp.int32),
            pltpu.VMEM((2, CHUNK + 8, LANES), jnp.int32),
            pltpu.SMEM((nb * 8, LANES), jnp.int32),
            pltpu.SMEM((2 * (CHUNK + 8), LANES), jnp.int32),
            pltpu.SMEM(front.shape, jnp.int32),
            pltpu.SemaphoreType.DMA((2,)),
            pltpu.SemaphoreType.DMA,
            pltpu.SemaphoreType.DMA,
        ],
        compiler_params=pltpu.CompilerParams(vmem_limit_bytes=40 * 1024 * 1024),
        cost_estimate=pl.CostEstimate(flops=200000000, bytes_accessed=100000000, transcendentals=0),
        name="neighbour_sums",
    )(feats, front, ids, nbr, wn, ws, dl, second)


def split_dot(ones, wide, dims):
    high = wide.astype(BF16)
    low = (wide - high.astype(F32)).astype(BF16)
    return lax.dot_general(ones, high, dims, preferred_element_type=F32) + lax.dot_general(
        ones, low, dims, preferred_element_type=F32
    )


NN = (((1,), (0,)), ((), ()))
TN = (((0,), (0,)), ((), ()))
NT = (((1,), (1,)), ((), ()))


def layers_kernel(
    nz, ny,
    part_ref, self_ref, deg_ref, w_ref, side_ref, b1_ref, w2s_ref, w2n_ref, b2_ref,
    logits_ref, gs_ref, gn_ref,
    grads_ref, gotw, sv, sall, got1, xs, got2, pre, got3, lp, got4, l2, got5,
    gp, gotg, gz, gotz, gall, gy,
    sw, rw, sf, rf, sa, ra, sb, rb, s0, r0, s1, r1, s2, r2, s3, r3, s4, r4, s5, r5,
    sg, rg, sz, rz, sq, rq, sy, ry, sx, rx, sh, rh,
):
    feat = lax.axis_index("feat")
    graph = lax.axis_index("graph")
    ng = part_ref.shape[0]
    z = feat // ny
    y = feat % ny
    core = graph % 2
    width = part_ref.shape[1] // 8
    cdim = w2s_ref.shape[0]
    rows = 2 * CLASSES // ng
    bit = rows // nz

    def at_graph(d):
        return (feat, (graph + d) % ng)

    def at_z(d):
        return (((z + d) % nz) * ny + y, graph)

    def at_y(d):
        return (z * ny + (y + d) % ny, graph)

    sibling = (feat, graph + 1 - 2 * core)

    barrier = pltpu.get_barrier_semaphore()
    for d in range(1, ng):
        pl.semaphore_signal(barrier, inc=1, device_id=at_graph(d), device_id_type=MESH)
    for d in range(1, nz):
        pl.semaphore_signal(barrier, inc=1, device_id=at_z(d), device_id_type=MESH)
    for d in range(1, ny):
        pl.semaphore_signal(barrier, inc=1, device_id=at_y(d), device_id_type=MESH)
    pl.semaphore_wait(barrier, (ng - 1) + (nz - 1) + (ny - 1))

    def remote(src, dst, ssem, rsem, where):
        return pltpu.make_async_remote_copy(
            src_ref=src, dst_ref=dst, send_sem=ssem, recv_sem=rsem,
            device_id=where, device_id_type=MESH,
        )

    def send(src, dst, ssem, rsem, where):
        copy = remote(src, dst, ssem, rsem, where)
        copy.start()
        return copy

    c1 = [
        send(part_ref.at[(graph + d) % ng], got1.at[d], s1.at[d], r1.at[d], at_graph(d))
        for d in range(1, ng)
    ]
    ca = [send(side_ref, sv.at[z], sa.at[d], ra.at[d], at_z(d)) for d in range(1, nz)]

    def weight_copy(d):
        return remote(w_ref, gotw.at[z], sw.at[d], rw.at[d], at_z(d))

    def weight_pass(d):
        block = gotw.at[(z - d + nz) % nz]
        return remote(block, block, sf.at[d], rf.at[d], sibling)

    @pl.when(z % 2 == core)
    def _():
        for d in range(1, nz):
            weight_copy(d).start()

    c0 = [
        send(
            self_ref.at[(z + d) % nz], got2.at[z, pl.ds(width, width)],
            s0.at[d], r0.at[d], at_z(d),
        )
        for d in range(1, nz)
    ]
    gotw[z] = w_ref[...]
    sv[z] = side_ref[...]
    got2[z, width : 2 * width, :] = self_ref[z]

    for c in ca:
        c.wait_recv()
    cb = [send(sv, sall.at[y], sb.at[d], rb.at[d], at_y(d)) for d in range(1, ny)]
    sall[y] = sv[...]

    summed = part_ref[graph].astype(F32)
    for d in range(1, ng):
        c1[d - 1].wait_recv()
        summed = summed + got1[d].astype(F32)
    for q in range(8):
        xs[q] = summed[q * width : (q + 1) * width] / deg_ref[:, q * LANES : (q + 1) * LANES]
    c2 = [
        send(
            xs.at[(z + d) % nz], got2.at[z, pl.ds(0, width)], s2.at[d], r2.at[d], at_z(d)
        )
        for d in range(1, nz)
    ]
    got2[z, 0:width, :] = xs[z]

    for d in range(1, nz):
        @pl.when((z + d) % 2 == core)
        def _():
            weight_copy(d).wait_recv()
            weight_pass(d).start()

    for c in cb:
        c.wait_recv()
    seeds = ny * nz * 8
    side = sall[...].reshape(seeds, side_ref.shape[1])
    dl = side[:, :CLASSES]
    second = side[:, CLASSES:].astype(jnp.int32)
    taken = lax.broadcasted_iota(jnp.int32, second.shape, 1) < FAN2
    deg2 = jnp.sum(jnp.where((second >= 0) & taken, 1.0, 0.0), axis=1, keepdims=True)
    spot = z * LANES + lax.broadcasted_iota(jnp.int32, (seeds, LANES), 1)
    hits = jnp.zeros((seeds, LANES), F32)
    for k in range(FAN2):
        hits = hits + jnp.where(second[:, k : k + 1] == spot, 1.0, 0.0)
    hits = hits.astype(BF16)
    at = lax.broadcasted_iota(jnp.int32, (seeds, LANES), 0)
    row = ((at // 8) % nz) * (ny * 8) + (at // (8 * nz)) * 8 + at % 8
    same = jnp.where(row == spot, 1.0, 0.0).astype(BF16)

    for c in c0 + c2:
        c.wait_recv()
    x = got2[...].reshape(nz * 2 * width, LANES)
    for d in range(1, nz):
        @pl.when((z + d) % 2 != core)
        def _():
            weight_pass(d).wait_recv()
    w = gotw[...].reshape(nz * 2 * width, w_ref.shape[1])
    high = x.astype(BF16)
    low = (x - high.astype(F32)).astype(BF16)
    part = lax.dot_general(high, w, TN, preferred_element_type=F32) + lax.dot_general(
        low, w, TN, preferred_element_type=F32
    )
    for k in range(ny):
        pre[k] = part[:, k * LANES : (k + 1) * LANES]
    c3 = [
        send(pre.at[(y + d) % ny], got3.at[d], s3.at[d], r3.at[d], at_y(d)) for d in range(1, ny)
    ]

    def exact(wide, ones):
        total = jnp.zeros((wide.shape[1], ones.shape[1]), F32)
        for _ in range(3):
            piece = wide.astype(BF16)
            total = total + lax.dot_general(piece, ones, TN, preferred_element_type=F32)
            wide = wide - piece.astype(F32)
        return total

    cot = jnp.concatenate([exact(dl, same), exact(dl / deg2, hits)], axis=0)
    cot_high = cot.astype(BF16)
    cot_low = (cot - cot_high.astype(F32)).astype(BF16)

    h = pre[y] + b1_ref[y]
    for d in range(1, ny):
        c3[d - 1].wait_recv()
        h = h + got3[d]
    h = jnp.maximum(h, 0.0).astype(BF16)

    g = jnp.dot(cot_high, h, preferred_element_type=F32) + jnp.dot(
        cot_low, h, preferred_element_type=F32
    )
    gp[...] = g.reshape(ng, rows, LANES)
    cg = [
        send(gp.at[(graph + d) % ng], gotg.at[d], sg.at[d], rg.at[d], at_graph(d))
        for d in range(1, ng)
    ]

    columns = pl.ds(pl.multiple_of(y * LANES, LANES), LANES)
    zs = lax.dot_general(h, w2s_ref[:, columns], NT, preferred_element_type=F32)
    zn = lax.dot_general(h, w2n_ref[:, columns], NT, preferred_element_type=F32)

    gsum = gp[graph]
    for d in range(1, ng):
        cg[d - 1].wait_recv()
        gsum = gsum + gotg[d]
    for k in range(nz):
        gz[k] = gsum[k * bit : (k + 1) * bit]
    cz = [send(gz.at[(z + d) % nz], gotz.at[d], sz.at[d], rz.at[d], at_z(d)) for d in range(1, nz)]

    scores = split_dot(hits, zn, NN) / deg2 + split_dot(same, zs, NN)
    lp[...] = scores.reshape(ny, nz, 8, cdim)
    c4 = [
        send(lp.at[(y + d) % ny], got4.at[d], s4.at[d], r4.at[d], at_y(d)) for d in range(1, ny)
    ]

    whole = gz[z]
    for d in range(1, nz):
        cz[d - 1].wait_recv()
        whole = whole + gotz[d]
    gall[z] = whole
    cq = [send(gall.at[z], gall.at[z], sq.at[d], rq.at[d], at_z(d)) for d in range(1, nz)]

    lsum = lp[y]
    for d in range(1, ny):
        c4[d - 1].wait_recv()
        lsum = lsum + got4[d]
    l2[...] = lsum
    c5 = [
        send(l2.at[(z + d) % nz], got5.at[d], s5.at[d], r5.at[d], at_z(d)) for d in range(1, nz)
    ]

    for c in cq:
        c.wait_recv()
    gy[y] = jnp.concatenate([gall[k] for k in range(nz)], axis=0)
    cy = [send(gy.at[y], gy.at[y], sy.at[d], ry.at[d], at_y(d)) for d in range(1, ny)]
    for c in cy:
        c.wait_recv()
    grads_ref[graph] = gy[...].reshape(ny * rows, LANES).astype(BF16)
    mine = grads_ref.at[graph]
    cx = [send(mine, mine, sx.at[d], rx.at[d], at_graph(2 * d)) for d in range(1, ng // 2)]
    ch = [send(mine, mine, sh.at[0], rh.at[0], sibling)]

    final = l2[z] + b2_ref[...]
    for d in range(1, nz):
        c5[d - 1].wait_recv()
        final = final + got5[d]
    logits_ref[...] = final

    for d in range(1, ng // 2):
        cx[d - 1].wait_recv()
        block = grads_ref.at[(graph + ng - 2 * d) % ng]
        ch.append(send(block, block, sh.at[d], rh.at[d], sibling))
    for c in ch:
        c.wait_recv()
    half = ng // 2
    for k in range(ng):
        out = gs_ref if k < half else gn_ref
        base = (k % half) * rows
        keep = min(rows, cdim - base)
        block = grads_ref[k].astype(F32)
        for j in range(ny):
            out[base : base + keep, j * LANES : (j + 1) * LANES] = block[
                j * rows : j * rows + keep
            ]
    for c in ca + cb + c0 + c1 + c2 + c3 + cg + c4 + cz + cq + c5 + cy + cx + ch:
        c.wait_send()

    @pl.when(z % 2 == core)
    def _():
        for d in range(1, nz):
            weight_copy(d).wait_send()

    for d in range(1, nz):
        @pl.when((z + d) % 2 == core)
        def _():
            weight_pass(d).wait_send()


def layers(nz, ny, part, own, deg, w, side, b1, w2s, w2n, b2):
    ng, rows, _ = part.shape
    width = rows // 8
    cdim = w2s.shape[0]
    cut = 2 * CLASSES // ng
    vmem = pl.BlockSpec(memory_space=pltpu.VMEM)
    dma = lambda n: pltpu.SemaphoreType.DMA((n,))
    pair = lambda n: [dma(n), dma(n)]
    return pl.pallas_call(
        functools.partial(layers_kernel, nz, ny),
        out_shape=(
            jax.ShapeDtypeStruct((8, cdim), F32),
            jax.ShapeDtypeStruct(w2s.shape, F32),
            jax.ShapeDtypeStruct(w2n.shape, F32),
        ),
        in_specs=[vmem] * 9,
        out_specs=(vmem, vmem, vmem),
        scratch_shapes=[
            pltpu.VMEM((ng, ny * cut, LANES), BF16),
            pltpu.VMEM((nz, 2 * width, w.shape[1]), BF16),
            pltpu.VMEM((nz,) + side.shape, F32),
            pltpu.VMEM((ny, nz) + side.shape, F32),
            pltpu.VMEM((ng, rows, LANES), BF16),
            pltpu.VMEM((8, width, LANES), F32),
            pltpu.VMEM((nz, 2 * width, LANES), F32),
            pltpu.VMEM((ny, LANES, LANES), F32),
            pltpu.VMEM((ny, LANES, LANES), F32),
            pltpu.VMEM((ny, nz, 8, cdim), F32),
            pltpu.VMEM((ny, nz, 8, cdim), F32),
            pltpu.VMEM((nz, 8, cdim), F32),
            pltpu.VMEM((nz, 8, cdim), F32),
            pltpu.VMEM((ng, cut, LANES), F32),
            pltpu.VMEM((ng, cut, LANES), F32),
            pltpu.VMEM((nz, cut // nz, LANES), F32),
            pltpu.VMEM((nz, cut // nz, LANES), F32),
            pltpu.VMEM((nz, cut // nz, LANES), F32),
            pltpu.VMEM((ny, cut, LANES), F32),
        ]
        + pair(nz) + pair(nz) + pair(nz) + pair(ny) + pair(nz) + pair(ng) + pair(nz)
        + pair(ny) + pair(ny) + pair(nz) + pair(ng) + pair(nz) + pair(nz) + pair(ny)
        + pair(ng) + pair(ng),
        compiler_params=pltpu.CompilerParams(
            collective_id=0, has_side_effects=True, vmem_limit_bytes=40 * 1024 * 1024
        ),
        cost_estimate=pl.CostEstimate(flops=300000000, bytes_accessed=10000000, transcendentals=0),
        name="layers",
    )(part, own, deg, w, side, b1, w2s, w2n, b2)


def on_device(feats, front_ids, nbr1, nbr2, w1_self, w1_neigh, b1, w2_self, w2_neigh, b2, dlogits):
    nb, targets, fan = nbr1.shape
    width, verts = feats.shape
    hidden, cdim = w2_self.shape
    nz, ny = 8, 4

    part, own, deg, w, side = gather(
        feats, front_ids.reshape(-1), front_ids[:, 0, :], nbr1.transpose(2, 0, 1),
        w1_neigh, w1_self,
        dlogits[0], nbr2[0], nb,
    )
    logits, grad_s, grad_n = layers(
        nz, ny, part, own, deg, w, side,
        b1.reshape(ny, 1, LANES), w2_self.T, w2_neigh.T, b2.reshape(1, cdim),
    )
    return (logits[None], grad_s.T, grad_n.T)


def solution(mesh):
    in_specs = (
        P("feat", "graph"),
        P(None, "graph", None),
        P(),
        P("graph", "feat", None),
        P("feat", None),
        P("feat", None),
        P(),
        P(),
        P(),
        P(),
        P("graph", "feat", None),
    )
    out_specs = (P("graph", "feat", None), P(), P())
    return jax.shard_map(
        on_device, mesh=mesh, in_specs=in_specs, out_specs=out_specs, check_vma=False
    )
```

```python
import functools

import jax
import jax.numpy as jnp
from jax import lax
from jax.experimental import pallas as pl
from jax.experimental.pallas import tpu as pltpu
from jax.sharding import PartitionSpec as P

LANES = 128
UNROLL = 4
BLOCK = 8
CHUNK = 32
CLASSES = 160
VMEM_BYTES = 60 * 1024 * 1024
FAN2 = 15
DENSE = 8
WORD_BITS = 15
WORD = 1 << WORD_BITS
MESH = pl.DeviceIdType.MESH
F32 = jnp.float32
BF16 = jnp.bfloat16
VALID = 1 << 29
RANK_AT = 18


def aligned(index, size):
    return pl.ds(pl.multiple_of(index * size, size), size)


def build_table(feats_ref, table):
    width, verts = feats_ref.shape

    def turn(i, c):
        block = feats_ref[:, aligned(i, LANES)].astype(F32)
        table[aligned(i, LANES), 0:width] = block.T
        return c

    lax.fori_loop(0, verts // LANES, turn, 0, unroll=16)
    table[verts : verts + 8, :] = jnp.zeros((8, LANES), F32)


def gather_kernel(
    nb, feats_hbm, front_ref, ids_hbm, nbr_hbm, wn_hbm, ws_hbm, dl_hbm, second_hbm,
    rest_ref, pairs_v, self_ref, deg_ref, w_ref, side_ref,
    table, acc, feats_ref, ids_ref, nbr_ref, wn_ref, ws_ref, dl_ref, second_ref, own, one, two, lists_v, lists_s, front_s,
    sems, front_sem, load_sems,
):
    width = feats_ref.shape[0]
    verts = feats_ref.shape[1]
    fan = nbr_ref.shape[0]
    per = fan * nb
    total = per * 8
    targets = 8 * LANES
    fs = front_ref.shape[0] // nb
    fs_bits = fs.bit_length() - 1
    graph = lax.axis_index("graph")

    load_nbr = pltpu.make_async_copy(nbr_hbm, nbr_ref, load_sems.at[0])
    load_nbr.start()
    load_ids = pltpu.make_async_copy(ids_hbm, ids_ref, load_sems.at[1])
    load_ids.start()
    load_feats = pltpu.make_async_copy(feats_hbm, feats_ref, load_sems.at[2])
    load_feats.start()
    small = [
        pltpu.make_async_copy(a, b, load_sems.at[3 + i])
        for i, (a, b) in enumerate(
            [(wn_hbm, wn_ref), (ws_hbm, ws_ref), (dl_hbm, dl_ref), (second_hbm, second_ref)]
        )
    ]
    for load in small:
        load.start()
    fetch = pltpu.make_async_copy(front_ref, front_s, front_sem)
    fetch.start()

    load_nbr.wait()
    degree = jnp.zeros((1, targets), F32)
    for k in range(fan):
        degree = degree + jnp.where(nbr_ref[k, pl.ds(graph, 1), :] >= 0, 1.0, 0.0)
    deg_ref[...] = degree

    part = (nb, targets)
    start = lax.broadcasted_iota(jnp.int32, part, 0) * fs
    tile = lax.broadcasted_iota(jnp.int32, part, 1) >> 7
    seen = jnp.zeros(part, jnp.int32)
    pair = [jnp.zeros(part, jnp.int32), jnp.zeros(part, jnp.int32)]
    for k in range(fan):
        ids = nbr_ref[k]
        here = (ids >> fs_bits) == graph
        local = ids & (fs - 1)
        for j in range(2):
            pair[j] = jnp.where(here & (seen == j), local, pair[j])
        entry = jnp.where(here & (seen > 1), VALID + (local + start) * 8 + tile, 0)
        for q in range(8):
            one[q * per + k * nb : q * per + (k + 1) * nb, :] = entry[
                :, q * LANES : (q + 1) * LANES
            ]
        seen = seen + jnp.where(here, 1, 0)
    load_ids.wait()
    for q in range(8):
        cut = slice(q * LANES, (q + 1) * LANES)
        found = [jnp.zeros((nb, LANES), jnp.int32), jnp.zeros((nb, LANES), jnp.int32)]
        for k in range(fs // LANES):
            line = ids_ref[:, 0, k * LANES : (k + 1) * LANES]
            for j in range(2):
                at = pair[j][:, cut]
                got = jnp.take_along_axis(line, at & (LANES - 1), axis=1)
                found[j] = jnp.where((at >> 7) == k, got, found[j])
        for j in range(2):
            found[j] = jnp.where(seen[:, cut] > j, found[j], verts)
        word = found[1] * WORD + found[0]
        for b in range(nb):
            pairs_v[b * 8 + q : b * 8 + q + 1, :] = word[b : b + 1]

    below = (
        lax.broadcasted_iota(jnp.int32, (per, per), 0)
        > lax.broadcasted_iota(jnp.int32, (per, per), 1)
    ).astype(F32).astype(BF16)
    lost = jnp.zeros((1, LANES), jnp.int32)
    for q in range(8):
        entry = one[q * per : (q + 1) * per, :]
        gone = jnp.where(entry == 0, 1.0, 0.0)
        before = jnp.dot(below, gone.astype(BF16), preferred_element_type=F32)
        rank = before.astype(jnp.int32) + lost
        one[q * per : (q + 1) * per, :] = jnp.where(entry == 0, 0, entry + rank * (1 << RANK_AT))
        lost = lost + jnp.sum(gone, axis=0, keepdims=True).astype(jnp.int32)
    count = total - lost

    src, dst = one, two
    bits = (total - 1).bit_length()
    block = 64
    for step in range(bits):
        far = 1 << step
        flag = 1 << (RANK_AT + step)
        for at in range(0, total, block):
            stay = src[at : at + block, :]
            have = max(0, min(block, total - at - far))
            kept = jnp.where((stay & flag) != 0, 0, stay)
            if have > 0:
                move = src[at + far : at + far + have, :]
                if have < block:
                    move = jnp.concatenate(
                        [move, jnp.zeros((block - have, LANES), jnp.int32)], axis=0
                    )
                kept = jnp.where((move & flag) != 0, move, kept)
            dst[at : at + block, :] = kept
        src, dst = dst, src

    lane_row = lax.broadcasted_iota(jnp.int32, (LANES, LANES), 1)
    key_row = jnp.broadcast_to(count * LANES, (LANES, LANES)) + lane_row
    key_col = key_row.astype(F32).T
    ahead = jnp.where(key_row.astype(F32) > key_col, 1.0, 0.0)
    place = jnp.sum(ahead, axis=1, keepdims=True).astype(jnp.int32)
    order = jnp.where(place == lane_row, 1.0, 0.0).astype(BF16)

    def shuffle(values):
        got = jnp.dot(values.astype(F32).astype(BF16), order, preferred_element_type=F32)
        return got.astype(jnp.int32)

    wide = jnp.broadcast_to(count, (8, LANES))
    sorted_count = (shuffle(wide // 64) * 64 + shuffle(wide % 64))[0:1]
    lane_id = shuffle(lax.broadcasted_iota(jnp.int32, (8, LANES), 1))[0:1]
    count_col = jnp.broadcast_to(sorted_count.astype(F32), (LANES, LANES)).T
    deepest = jnp.max(count)
    chunks = (deepest + CHUNK - 1) // CHUNK

    def prepare(ch, slot):
        entries = src[aligned(ch, CHUNK), :]
        ident = (entries >> 3) & (nb * fs - 1)
        ident = shuffle(ident >> 8) * 256 + shuffle(ident & 255)
        group = shuffle(entries & 7)
        at_row = ch * CHUNK + lax.broadcasted_iota(jnp.int32, (CHUNK, LANES), 0)
        live = sorted_count > at_row
        goal = (ident >> fs_bits) * targets + group * LANES + lane_id
        word = jnp.where(live, goal * WORD + ident, nb * targets * WORD)
        lists_v[slot, 0:CHUNK, :] = word
        row_at = (ch * CHUNK + lane_row).astype(F32)
        in_row = jnp.sum(jnp.where(count_col > row_at, 1.0, 0.0), axis=0, keepdims=True)
        groups = (in_row.astype(jnp.int32) + (UNROLL - 1)) // UNROLL
        lists_v[slot, CHUNK : CHUNK + 8, :] = jnp.broadcast_to(groups, (8, LANES))

    def transfer(slot):
        return pltpu.make_async_copy(
            lists_v.at[slot],
            lists_s.at[pl.ds(pl.multiple_of(slot * (CHUNK + 8), 8), CHUNK + 8)],
            sems.at[slot],
        )

    @pl.when(chunks > 0)
    def _():
        prepare(0, 0)
        transfer(0).start()

    for load in small:
        load.wait()
    w_ref[...] = jnp.concatenate(
        [wn_ref[...].astype(F32), ws_ref[...].astype(F32)], axis=0
    ).astype(BF16)
    side_ref[...] = jnp.zeros_like(side_ref)
    side_ref[:, 0 : dl_ref.shape[1]] = dl_ref[...]
    side_ref[:, CLASSES : CLASSES + second_ref.shape[1]] = second_ref[...].astype(F32)
    load_feats.wait()

    build_table(feats_ref, table)


    def clear(i, c):
        acc[aligned(i, 8), :] = jnp.zeros((8, LANES), F32)
        return c

    lax.fori_loop(0, acc.shape[0] // 8, clear, 0, unroll=25)

    fetch.wait()

    def chunk(ch, c):
        slot = ch & 1
        base = slot * (CHUNK + 8)
        transfer(slot).wait()

        @pl.when(ch + 1 < chunks)
        def _():
            prepare(ch + 1, 1 - slot)
            transfer(1 - slot).start()

        def row(r, c):
            def group(g):
                words = [lists_s[at, g * UNROLL + u] for u in range(UNROLL)]
                got = [table[pl.ds(front_s[w & (WORD - 1)], 1), :] for w in words]
                goals = [w >> WORD_BITS for w in words]
                old = [acc[pl.ds(a, 1), :] for a in goals]
                for u in range(UNROLL):
                    acc[pl.ds(goals[u], 1), :] = got[u] + old[u]

            groups = lists_s[base + CHUNK, r]
            at = base + r

            def block(h):
                for g in range(h * BLOCK, (h + 1) * BLOCK):
                    group(g)

            for h in range(LANES // UNROLL // BLOCK):
                pl.when(h * BLOCK < groups)(functools.partial(block, h))
            return c

        return lax.fori_loop(0, jnp.minimum(CHUNK, deepest - ch * CHUNK), row, c)

    lax.fori_loop(0, chunks, chunk, 0)

    def mine(i, c):
        base = graph * fs + i * UNROLL
        got = [table[pl.ds(front_s[base + u], 1), :] for u in range(UNROLL)]
        for u in range(UNROLL):
            own[pl.ds(i * UNROLL + u, 1), :] = got[u]
        return c

    lax.fori_loop(0, targets // UNROLL, mine, 0)

    for b in range(nb):
        turned = [
            acc[b * targets + q * LANES : b * targets + (q + 1) * LANES, 0:width].T
            for q in range(8)
        ]
        rest_ref[b] = jnp.concatenate(turned, axis=0)
    for q in range(8):
        self_ref[q] = own[q * LANES : (q + 1) * LANES, 0:width].T


def gather(feats, front, ids, nbr, wn, ws, dl, second, nb):
    width, verts = feats.shape
    total = nbr.shape[0] * nb * 8
    vmem = pl.BlockSpec(memory_space=pltpu.VMEM)
    return pl.pallas_call(
        functools.partial(gather_kernel, nb),
        out_shape=(
            jax.ShapeDtypeStruct((nb, 8 * width, LANES), F32),
            jax.ShapeDtypeStruct((nb * 8, LANES), jnp.int32),
            jax.ShapeDtypeStruct((8, width, LANES), F32),
            jax.ShapeDtypeStruct((1, 8 * LANES), F32),
            jax.ShapeDtypeStruct((2 * width, wn.shape[1]), BF16),
            jax.ShapeDtypeStruct((8, CLASSES + 16), F32),
        ),
        in_specs=[pl.BlockSpec(memory_space=pltpu.HBM)] * 8,
        out_specs=(vmem,) * 6,
        scratch_shapes=[
            pltpu.VMEM((verts + 8, LANES), F32),
            pltpu.VMEM((nb * 8 * LANES + 8, LANES), F32),
            pltpu.VMEM(feats.shape, BF16),
            pltpu.VMEM(ids.shape, jnp.int32),
            pltpu.VMEM(nbr.shape, jnp.int32),
            pltpu.VMEM(wn.shape, BF16),
            pltpu.VMEM(ws.shape, BF16),
            pltpu.VMEM(dl.shape, F32),
            pltpu.VMEM(second.shape, jnp.int32),
            pltpu.VMEM((8 * LANES, LANES), F32),
            pltpu.VMEM((total + 64, LANES), jnp.int32),
            pltpu.VMEM((total + 64, LANES), jnp.int32),
            pltpu.VMEM((2, CHUNK + 8, LANES), jnp.int32),
            pltpu.SMEM((2 * (CHUNK + 8), LANES), jnp.int32),
            pltpu.SMEM(front.shape, jnp.int32),
            pltpu.SemaphoreType.DMA((2,)),
            pltpu.SemaphoreType.DMA,
            pltpu.SemaphoreType.DMA((7,)),
        ],
        compiler_params=pltpu.CompilerParams(vmem_limit_bytes=VMEM_BYTES),
        cost_estimate=pl.CostEstimate(flops=200000000, bytes_accessed=100000000, transcendentals=0),
        name="neighbour_sums",
    )(feats, front, ids, nbr, wn, ws, dl, second)


def split_dot(ones, wide, dims):
    high = wide.astype(BF16)
    low = (wide - high.astype(F32)).astype(BF16)
    return lax.dot_general(ones, high, dims, preferred_element_type=F32) + lax.dot_general(
        ones, low, dims, preferred_element_type=F32
    )


NN = (((1,), (0,)), ((), ()))
TN = (((0,), (0,)), ((), ()))
NT = (((1,), (1,)), ((), ()))


def layers_kernel(
    nz, ny,
    feats_hbm, rest_hbm, pairs_hbm, self_hbm, deg_hbm, w_hbm, side_hbm,
    b1_hbm, w2s_hbm, w2n_hbm, b2_hbm,
    out_ref,
    feats_ref, table, rest, self_ref, deg_ref, w_ref, side_ref,
    b1_ref, w2s_ref, w2n_ref, b2_ref, load_sems, pairs_s, sums, part_ref, grads_ref, gotw, sv, sall, got1, xs, got2, pre, got3, lp, got4, l2, got5,
    gp, gotg, gx, gotx, gz, gy,
    sw, rw, sf, rf, sa, ra, sb, rb, s0, r0, s1, r1, s2, r2, s3, r3, s4, r4, s5, r5,
    sg, rg, sz, rz, sy, ry, sx, rx, sh, rh,
):
    feat = lax.axis_index("feat")
    graph = lax.axis_index("graph")
    ng = pairs_hbm.shape[0] // 8
    z = feat // ny
    y = feat % ny
    core = graph % 2
    width = self_ref.shape[1]
    cdim = w2s_ref.shape[0]
    rows = 2 * CLASSES // ng
    nx = ng // 2
    xat = graph // 2

    def at_graph(d):
        return (feat, (graph + d) % ng)

    def at_x(d):
        return (feat, (graph + 2 * d) % ng)

    def at_z(d):
        return (((z + d) % nz) * ny + y, graph)

    def at_y(d):
        return (z * ny + (y + d) % ny, graph)

    sibling = (feat, graph + 1 - 2 * core)

    moved = [
        (feats_hbm, feats_ref), (w_hbm, w_ref), (side_hbm, side_ref), (self_hbm, self_ref),
        (pairs_hbm, pairs_s), (rest_hbm, rest), (deg_hbm, deg_ref), (b1_hbm, b1_ref),
        (w2s_hbm, w2s_ref), (w2n_hbm, w2n_ref), (b2_hbm, b2_ref),
    ]
    loads = [pltpu.make_async_copy(a, b, load_sems.at[i]) for i, (a, b) in enumerate(moved)]
    for load in loads:
        load.start()

    barrier = pltpu.get_barrier_semaphore()
    for d in range(1, ng):
        pl.semaphore_signal(barrier, inc=1, device_id=at_graph(d), device_id_type=MESH)
    for d in range(1, nz):
        pl.semaphore_signal(barrier, inc=1, device_id=at_z(d), device_id_type=MESH)
    for d in range(1, ny):
        pl.semaphore_signal(barrier, inc=1, device_id=at_y(d), device_id_type=MESH)

    targets = 8 * LANES

    def batch_sums(d):
        b = (graph + d) % ng

        def tile(q, c):
            r = b * 8 + q
            into = pl.multiple_of(q * LANES, LANES)
            for at in range(0, LANES, DENSE):
                words = [pairs_s[r, at + u] for u in range(DENSE)]
                got = [
                    table[pl.ds(w & (WORD - 1), 1), :]
                    + table[pl.ds(w >> WORD_BITS, 1), :]
                    for w in words
                ]
                for u in range(DENSE):
                    sums[pl.ds(into + at + u, 1), :] = got[u]
            return c

        lax.fori_loop(0, 8, tile, 0)
        turned = [sums[q * LANES : (q + 1) * LANES, 0:width].T for q in range(8)]
        part_ref[b] = (jnp.concatenate(turned, axis=0) + rest[b]).astype(BF16)

    loads[0].wait()
    build_table(feats_ref, table)
    for load in loads[1:4]:
        load.wait()
    pl.semaphore_wait(barrier, (ng - 1) + (nz - 1) + (ny - 1))

    def remote(src, dst, ssem, rsem, where):
        return pltpu.make_async_remote_copy(
            src_ref=src, dst_ref=dst, send_sem=ssem, recv_sem=rsem,
            device_id=where, device_id_type=MESH,
        )

    def send(src, dst, ssem, rsem, where):
        copy = remote(src, dst, ssem, rsem, where)
        copy.start()
        return copy

    far = nz // 2

    def weight_copy(k):
        to = ((z + (1 - 2 * core) * k + nz) % nz) * ny + y
        return remote(w_ref, gotw.at[z], sw.at[k], rw.at[k], (to, graph))

    def weight_pass(k):
        block = gotw.at[(z - (1 - 2 * core) * k + nz) % nz]
        return remote(block, block, sf.at[k], rf.at[k], sibling)

    def weight_step(k):
        def step():
            weight_copy(k).wait_recv()
            weight_pass(k).start()

        if k < far:
            step()
        else:
            pl.when(core == 0)(step)

    for k in range(1, far):
        weight_copy(k).start()
    pl.when(core == 0)(lambda: weight_copy(far).start())
    gotw[z] = w_ref[...]

    c0 = [
        send(
            self_ref.at[(z + d) % nz], got2.at[z, pl.ds(width, width)],
            s0.at[d], r0.at[d], at_z(d),
        )
        for d in range(1, nz)
    ]
    sv[z] = side_ref[...]
    got2[z, width : 2 * width, :] = self_ref[z]

    ca = [send(side_ref, sv.at[z], sa.at[d], ra.at[d], at_z(d)) for d in range(1, nz)]

    for load in loads[4:]:
        load.wait()
    batch_sums(1)
    c1 = []
    for d in range(1, ng):
        c1.append(
            send(part_ref.at[(graph + d) % ng], got1.at[d], s1.at[d], r1.at[d], at_graph(d))
        )
        batch_sums((d + 1) % ng)

    summed = part_ref[graph].astype(F32)
    for d in range(1, ng):
        c1[d - 1].wait_recv()
        summed = summed + got1[d].astype(F32)
    for q in range(8):
        xs[q] = summed[q * width : (q + 1) * width] / deg_ref[:, q * LANES : (q + 1) * LANES]
    c2 = [
        send(
            xs.at[(z + d) % nz], got2.at[z, pl.ds(0, width)], s2.at[d], r2.at[d], at_z(d)
        )
        for d in range(1, nz)
    ]
    got2[z, 0:width, :] = xs[z]
    for c in ca:
        c.wait_recv()
    cb = [send(sv, sall.at[y], sb.at[d], rb.at[d], at_y(d)) for d in range(1, ny)]
    sall[y] = sv[...]
    for k in range(1, far + 1):
        weight_step(k)

    for c in c0 + c2:
        c.wait_recv()
    x = got2[...].reshape(nz * 2 * width, LANES)
    for k in range(1, far):
        weight_pass(k).wait_recv()
    pl.when(core == 1)(lambda: weight_pass(far).wait_recv())
    w = gotw[...].reshape(nz * 2 * width, w_ref.shape[1])
    high = x.astype(BF16)
    low = (x - high.astype(F32)).astype(BF16)
    part = lax.dot_general(high, w, TN, preferred_element_type=F32) + lax.dot_general(
        low, w, TN, preferred_element_type=F32
    )
    for k in range(ny):
        pre[k] = part[:, k * LANES : (k + 1) * LANES]
    c3 = [
        send(pre.at[(y + d) % ny], got3.at[d], s3.at[d], r3.at[d], at_y(d)) for d in range(1, ny)
    ]

    for c in cb:
        c.wait_recv()
    seeds = ny * nz * 8
    side = sall[...].reshape(seeds, side_ref.shape[1])
    dl = side[:, :CLASSES]
    second = side[:, CLASSES:].astype(jnp.int32)
    taken = lax.broadcasted_iota(jnp.int32, second.shape, 1) < FAN2
    deg2 = jnp.sum(jnp.where((second >= 0) & taken, 1.0, 0.0), axis=1, keepdims=True)
    spot = z * LANES + lax.broadcasted_iota(jnp.int32, (seeds, LANES), 1)
    hits = jnp.zeros((seeds, LANES), F32)
    for k in range(FAN2):
        hits = hits + jnp.where(second[:, k : k + 1] == spot, 1.0, 0.0)
    hits = hits.astype(BF16)
    at = lax.broadcasted_iota(jnp.int32, (seeds, LANES), 0)
    row = ((at // 8) % nz) * (ny * 8) + (at // (8 * nz)) * 8 + at % 8
    same = jnp.where(row == spot, 1.0, 0.0).astype(BF16)

    def exact(wide, ones):
        total = jnp.zeros((wide.shape[1], ones.shape[1]), F32)
        for _ in range(3):
            piece = wide.astype(BF16)
            total = total + lax.dot_general(piece, ones, TN, preferred_element_type=F32)
            wide = wide - piece.astype(F32)
        return total

    cot = jnp.concatenate([exact(dl, same), exact(dl / deg2, hits)], axis=0)
    cot_high = cot.astype(BF16)
    cot_low = (cot - cot_high.astype(F32)).astype(BF16)

    h = pre[y] + b1_ref[y]
    for d in range(1, ny):
        c3[d - 1].wait_recv()
        h = h + got3[d]
    h = jnp.maximum(h, 0.0).astype(BF16)

    g = jnp.dot(cot_high, h, preferred_element_type=F32) + jnp.dot(
        cot_low, h, preferred_element_type=F32
    )
    gp[...] = g.reshape(nx, 2, rows, LANES)
    cg = [send(gp.at[:, 1 - core], gotg, sg.at[0], rg.at[0], sibling)]
    cg[0].wait_recv()
    gx[...] = gp[:, core] + gotg[...]
    for d in range(1, nx):
        cg.append(send(gx.at[(xat + d) % nx], gotx.at[d], sg.at[d], rg.at[d], at_x(d)))

    columns = pl.ds(pl.multiple_of(y * LANES, LANES), LANES)
    zs = lax.dot_general(h, w2s_ref[:, columns], NT, preferred_element_type=F32)
    zn = lax.dot_general(h, w2n_ref[:, columns], NT, preferred_element_type=F32)

    gsum = gx[xat]
    for d in range(1, nx):
        cg[d].wait_recv()
        gsum = gsum + gotx[d]
    gz[z] = gsum
    cz = [send(gz.at[z], gz.at[z], sz.at[d], rz.at[d], at_z(d)) for d in range(1, nz)]

    scores = split_dot(hits, zn, NN) / deg2 + split_dot(same, zs, NN)
    lp[...] = scores.reshape(ny, nz, 8, cdim)
    c4 = [
        send(lp.at[(y + d) % ny], got4.at[d], s4.at[d], r4.at[d], at_y(d)) for d in range(1, ny)
    ]

    for c in cz:
        c.wait_recv()
    whole = gz[0]
    for k in range(1, nz):
        whole = whole + gz[k]
    gy[y] = whole
    cy = [send(gy.at[y], gy.at[y], sy.at[d], ry.at[d], at_y(d)) for d in range(1, ny)]

    lsum = lp[y]
    for d in range(1, ny):
        c4[d - 1].wait_recv()
        lsum = lsum + got4[d]
    l2[...] = lsum
    c5 = [
        send(l2.at[(z + d) % nz], got5.at[d], s5.at[d], r5.at[d], at_z(d)) for d in range(1, nz)
    ]

    for c in cy:
        c.wait_recv()
    grads_ref[core, xat] = gy[...].reshape(ny * rows, LANES).astype(BF16)
    mine = grads_ref.at[core, xat]
    cx = [send(mine, mine, sx.at[d], rx.at[d], at_x(d)) for d in range(1, nx)]

    final = l2[z] + b2_ref[...]
    for d in range(1, nz):
        c5[d - 1].wait_recv()
        final = final + got5[d]
    out_ref[2 * CLASSES : 2 * CLASSES + 8, 0:cdim] = final

    for c in cx:
        c.wait_recv()
    mine = grads_ref.at[core]
    ch = [send(mine, mine, sh.at[0], rh.at[0], sibling)]
    ch[0].wait_recv()
    for k in range(ng):
        block = grads_ref[k % 2, k // 2].astype(F32)
        for j in range(ny):
            out_ref[k * rows : (k + 1) * rows, j * LANES : (j + 1) * LANES] = block[
                j * rows : (j + 1) * rows
            ]
    for c in ca + cb + c0 + c1 + c2 + c3 + cg + c4 + cz + c5 + cy + cx + ch:
        c.wait_send()

    for k in range(1, far):
        weight_copy(k).wait_send()
        weight_pass(k).wait_send()

    @pl.when(core == 0)
    def _():
        weight_copy(far).wait_send()
        weight_pass(far).wait_send()


def layers(nz, ny, feats, rest, pairs, own, deg, w, side, b1, w2s, w2n, b2):
    ng = pairs.shape[0] // 8
    width = own.shape[1]
    rows = 8 * width
    cdim = w2s.shape[0]
    cut = 2 * CLASSES // ng
    vmem = pl.BlockSpec(memory_space=pltpu.VMEM)
    dma = lambda n: pltpu.SemaphoreType.DMA((n,))
    pair = lambda n: [dma(n), dma(n)]
    return pl.pallas_call(
        functools.partial(layers_kernel, nz, ny),
        out_shape=jax.ShapeDtypeStruct((2 * CLASSES + 8, w2s.shape[1]), F32),
        in_specs=[pl.BlockSpec(memory_space=pltpu.HBM)] * 11,
        out_specs=vmem,
        scratch_shapes=[
            pltpu.VMEM(feats.shape, BF16),
            pltpu.VMEM((feats.shape[1] + 8, LANES), F32),
            pltpu.VMEM(rest.shape, F32),
            pltpu.VMEM(own.shape, F32),
            pltpu.VMEM(deg.shape, F32),
            pltpu.VMEM(w.shape, BF16),
            pltpu.VMEM(side.shape, F32),
            pltpu.VMEM(b1.shape, F32),
            pltpu.VMEM(w2s.shape, BF16),
            pltpu.VMEM(w2n.shape, BF16),
            pltpu.VMEM(b2.shape, F32),
            pltpu.SemaphoreType.DMA((11,)),
            pltpu.SMEM(pairs.shape, jnp.int32),
            pltpu.VMEM((8 * LANES, LANES), F32),
            pltpu.VMEM((ng, rows, LANES), BF16),
            pltpu.VMEM((2, ng // 2, ny * cut, LANES), BF16),
            pltpu.VMEM((nz, 2 * width, w.shape[1]), BF16),
            pltpu.VMEM((nz,) + side.shape, F32),
            pltpu.VMEM((ny, nz) + side.shape, F32),
            pltpu.VMEM((ng, rows, LANES), BF16),
            pltpu.VMEM((8, width, LANES), F32),
            pltpu.VMEM((nz, 2 * width, LANES), F32),
            pltpu.VMEM((ny, LANES, LANES), F32),
            pltpu.VMEM((ny, LANES, LANES), F32),
            pltpu.VMEM((ny, nz, 8, cdim), F32),
            pltpu.VMEM((ny, nz, 8, cdim), F32),
            pltpu.VMEM((nz, 8, cdim), F32),
            pltpu.VMEM((nz, 8, cdim), F32),
            pltpu.VMEM((ng // 2, 2, cut, LANES), F32),
            pltpu.VMEM((ng // 2, cut, LANES), F32),
            pltpu.VMEM((ng // 2, cut, LANES), F32),
            pltpu.VMEM((ng // 2, cut, LANES), F32),
            pltpu.VMEM((nz, cut, LANES), F32),
            pltpu.VMEM((ny, cut, LANES), F32),
        ]
        + pair(nz) + pair(nz) + pair(nz) + pair(ny) + pair(nz) + pair(ng) + pair(nz)
        + pair(ny) + pair(ny) + pair(nz) + pair(ng) + pair(nz) + pair(ny) + pair(ng) + pair(1),
        compiler_params=pltpu.CompilerParams(
            collective_id=0, has_side_effects=True, vmem_limit_bytes=VMEM_BYTES
        ),
        cost_estimate=pl.CostEstimate(flops=300000000, bytes_accessed=10000000, transcendentals=0),
        name="layers",
    )(feats, rest, pairs, own, deg, w, side, b1, w2s, w2n, b2)


def on_device(feats, front_ids, nbr1, nbr2, w1_self, w1_neigh, b1, w2_self, w2_neigh, b2, dlogits):
    nb, targets, fan = nbr1.shape
    width, verts = feats.shape
    hidden, cdim = w2_self.shape
    nz, ny = 8, 4

    rest, pairs, own, deg, w, side = gather(
        feats, front_ids.reshape(-1), front_ids, nbr1.transpose(2, 0, 1),
        w1_neigh, w1_self,
        dlogits[0], nbr2[0], nb,
    )
    out = layers(
        nz, ny, feats, rest, pairs, own, deg, w, side,
        b1.reshape(ny, 1, LANES), w2_self.T, w2_neigh.T, b2.reshape(1, cdim),
    )
    return (
        out[None, 2 * CLASSES :, :cdim],
        out[:cdim].T,
        out[CLASSES : CLASSES + cdim].T,
    )


def solution(mesh):
    in_specs = (
        P("feat", "graph"),
        P(None, "graph", None),
        P(),
        P("graph", "feat", None),
        P("feat", None),
        P("feat", None),
        P(),
        P(),
        P(),
        P(),
        P("graph", "feat", None),
    )
    out_specs = (P("graph", "feat", None), P(), P())
    return jax.shard_map(
        on_device, mesh=mesh, in_specs=in_specs, out_specs=out_specs, check_vma=False
    )
```

```python
import functools

import jax
import jax.numpy as jnp
from jax import lax
from jax.experimental import pallas as pl
from jax.experimental.pallas import tpu as pltpu
from jax.sharding import PartitionSpec as P

LANES = 128
UNROLL = 4
BLOCK = 8
CHUNK = 32
CLASSES = 160
VMEM_BYTES = 60 * 1024 * 1024
FAN2 = 15
DENSE = 8
OWN = 16
WORD_BITS = 15
WORD = 1 << WORD_BITS
MESH = pl.DeviceIdType.MESH
F32 = jnp.float32
BF16 = jnp.bfloat16
VALID = 1 << 29
RANK_AT = 18


def aligned(index, size):
    return pl.ds(pl.multiple_of(index * size, size), size)


def build_table(feats_ref, table):
    width, verts = feats_ref.shape

    def turn(i, c):
        block = feats_ref[:, aligned(i, LANES)].astype(F32)
        table[aligned(i, LANES), 0:width] = block.T
        return c

    lax.fori_loop(0, verts // LANES, turn, 0, unroll=16)
    table[verts : verts + 8, :] = jnp.zeros((8, LANES), F32)


def gather_kernel(
    nb, feats_hbm, front_ref, ids_hbm, nbr_hbm, wn_hbm, ws_hbm, dl_hbm, second_hbm,
    rest_ref, pairs_v, deg_ref, w_ref, side_ref,
    table, acc, feats_ref, ids_ref, nbr_ref, wn_ref, ws_ref, dl_ref, second_ref, one, two, lists_v, lists_s, front_s,
    sems, front_sem, load_sems,
):
    width = feats_ref.shape[0]
    verts = feats_ref.shape[1]
    fan = nbr_ref.shape[0]
    per = fan * nb
    total = per * 8
    targets = 8 * LANES
    fs = front_ref.shape[0] // nb
    fs_bits = fs.bit_length() - 1
    graph = lax.axis_index("graph")

    load_nbr = pltpu.make_async_copy(nbr_hbm, nbr_ref, load_sems.at[0])
    load_nbr.start()
    load_ids = pltpu.make_async_copy(ids_hbm, ids_ref, load_sems.at[1])
    load_ids.start()
    load_feats = pltpu.make_async_copy(feats_hbm, feats_ref, load_sems.at[2])
    load_feats.start()
    small = [
        pltpu.make_async_copy(a, b, load_sems.at[3 + i])
        for i, (a, b) in enumerate(
            [(wn_hbm, wn_ref), (ws_hbm, ws_ref), (dl_hbm, dl_ref), (second_hbm, second_ref)]
        )
    ]
    for load in small:
        load.start()
    fetch = pltpu.make_async_copy(front_ref, front_s, front_sem)
    fetch.start()

    load_nbr.wait()
    degree = jnp.zeros((1, targets), F32)
    for k in range(fan):
        degree = degree + jnp.where(nbr_ref[k, pl.ds(graph, 1), :] >= 0, 1.0, 0.0)
    deg_ref[...] = degree

    part = (nb, targets)
    start = lax.broadcasted_iota(jnp.int32, part, 0) * fs
    tile = lax.broadcasted_iota(jnp.int32, part, 1) >> 7
    seen = jnp.zeros(part, jnp.int32)
    pair = [jnp.zeros(part, jnp.int32), jnp.zeros(part, jnp.int32)]
    for k in range(fan):
        ids = nbr_ref[k]
        here = (ids >> fs_bits) == graph
        local = ids & (fs - 1)
        for j in range(2):
            pair[j] = jnp.where(here & (seen == j), local, pair[j])
        entry = jnp.where(here & (seen > 1), VALID + (local + start) * 8 + tile, 0)
        for q in range(8):
            one[q * per + k * nb : q * per + (k + 1) * nb, :] = entry[
                :, q * LANES : (q + 1) * LANES
            ]
        seen = seen + jnp.where(here, 1, 0)
    load_ids.wait()
    for q in range(8):
        cut = slice(q * LANES, (q + 1) * LANES)
        found = [jnp.zeros((nb, LANES), jnp.int32), jnp.zeros((nb, LANES), jnp.int32)]
        for k in range(fs // LANES):
            line = ids_ref[:, 0, k * LANES : (k + 1) * LANES]
            for j in range(2):
                at = pair[j][:, cut]
                got = jnp.take_along_axis(line, at & (LANES - 1), axis=1)
                found[j] = jnp.where((at >> 7) == k, got, found[j])
        for j in range(2):
            found[j] = jnp.where(seen[:, cut] > j, found[j], verts)
        word = found[1] * WORD + found[0]
        for b in range(nb):
            pairs_v[b * 8 + q : b * 8 + q + 1, :] = word[b : b + 1]

    below = (
        lax.broadcasted_iota(jnp.int32, (per, per), 0)
        > lax.broadcasted_iota(jnp.int32, (per, per), 1)
    ).astype(F32).astype(BF16)
    lost = jnp.zeros((1, LANES), jnp.int32)
    for q in range(8):
        entry = one[q * per : (q + 1) * per, :]
        gone = jnp.where(entry == 0, 1.0, 0.0)
        before = jnp.dot(below, gone.astype(BF16), preferred_element_type=F32)
        rank = before.astype(jnp.int32) + lost
        one[q * per : (q + 1) * per, :] = jnp.where(entry == 0, 0, entry + rank * (1 << RANK_AT))
        lost = lost + jnp.sum(gone, axis=0, keepdims=True).astype(jnp.int32)
    count = total - lost

    src, dst = one, two
    bits = (total - 1).bit_length()
    block = 64
    for step in range(bits):
        far = 1 << step
        flag = 1 << (RANK_AT + step)
        for at in range(0, total, block):
            stay = src[at : at + block, :]
            have = max(0, min(block, total - at - far))
            kept = jnp.where((stay & flag) != 0, 0, stay)
            if have > 0:
                move = src[at + far : at + far + have, :]
                if have < block:
                    move = jnp.concatenate(
                        [move, jnp.zeros((block - have, LANES), jnp.int32)], axis=0
                    )
                kept = jnp.where((move & flag) != 0, move, kept)
            dst[at : at + block, :] = kept
        src, dst = dst, src

    lane_row = lax.broadcasted_iota(jnp.int32, (LANES, LANES), 1)
    key_row = jnp.broadcast_to(count * LANES, (LANES, LANES)) + lane_row
    key_col = key_row.astype(F32).T
    ahead = jnp.where(key_row.astype(F32) > key_col, 1.0, 0.0)
    place = jnp.sum(ahead, axis=1, keepdims=True).astype(jnp.int32)
    order = jnp.where(place == lane_row, 1.0, 0.0).astype(BF16)

    def shuffle(values):
        got = jnp.dot(values.astype(F32).astype(BF16), order, preferred_element_type=F32)
        return got.astype(jnp.int32)

    wide = jnp.broadcast_to(count, (8, LANES))
    sorted_count = (shuffle(wide // 64) * 64 + shuffle(wide % 64))[0:1]
    lane_id = shuffle(lax.broadcasted_iota(jnp.int32, (8, LANES), 1))[0:1]
    count_col = jnp.broadcast_to(sorted_count.astype(F32), (LANES, LANES)).T
    deepest = jnp.max(count)
    chunks = (deepest + CHUNK - 1) // CHUNK

    def prepare(ch, slot):
        entries = src[aligned(ch, CHUNK), :]
        ident = (entries >> 3) & (nb * fs - 1)
        ident = shuffle(ident >> 8) * 256 + shuffle(ident & 255)
        group = shuffle(entries & 7)
        at_row = ch * CHUNK + lax.broadcasted_iota(jnp.int32, (CHUNK, LANES), 0)
        live = sorted_count > at_row
        goal = (ident >> fs_bits) * targets + group * LANES + lane_id
        word = jnp.where(live, goal * WORD + ident, nb * targets * WORD)
        lists_v[slot, 0:CHUNK, :] = word
        row_at = (ch * CHUNK + lane_row).astype(F32)
        in_row = jnp.sum(jnp.where(count_col > row_at, 1.0, 0.0), axis=0, keepdims=True)
        groups = (in_row.astype(jnp.int32) + (UNROLL - 1)) // UNROLL
        lists_v[slot, CHUNK : CHUNK + 8, :] = jnp.broadcast_to(groups, (8, LANES))

    def transfer(slot):
        return pltpu.make_async_copy(
            lists_v.at[slot],
            lists_s.at[pl.ds(pl.multiple_of(slot * (CHUNK + 8), 8), CHUNK + 8)],
            sems.at[slot],
        )

    @pl.when(chunks > 0)
    def _():
        prepare(0, 0)
        transfer(0).start()

    for load in small:
        load.wait()
    w_ref[...] = jnp.concatenate(
        [wn_ref[...].astype(F32), ws_ref[...].astype(F32)], axis=0
    ).astype(BF16)
    side_ref[...] = jnp.zeros_like(side_ref)
    side_ref[:, 0 : dl_ref.shape[1]] = dl_ref[...]
    side_ref[:, CLASSES : CLASSES + second_ref.shape[1]] = second_ref[...].astype(F32)
    load_feats.wait()

    build_table(feats_ref, table)


    def clear(i, c):
        acc[aligned(i, 8), :] = jnp.zeros((8, LANES), F32)
        return c

    lax.fori_loop(0, acc.shape[0] // 8, clear, 0, unroll=25)

    fetch.wait()

    def chunk(ch, c):
        slot = ch & 1
        base = slot * (CHUNK + 8)
        transfer(slot).wait()

        @pl.when(ch + 1 < chunks)
        def _():
            prepare(ch + 1, 1 - slot)
            transfer(1 - slot).start()

        def row(r, c):
            def group(g):
                words = [lists_s[at, g * UNROLL + u] for u in range(UNROLL)]
                got = [table[pl.ds(front_s[w & (WORD - 1)], 1), :] for w in words]
                goals = [w >> WORD_BITS for w in words]
                old = [acc[pl.ds(a, 1), :] for a in goals]
                for u in range(UNROLL):
                    acc[pl.ds(goals[u], 1), :] = got[u] + old[u]

            groups = lists_s[base + CHUNK, r]
            at = base + r

            def block(h):
                for g in range(h * BLOCK, (h + 1) * BLOCK):
                    group(g)

            for h in range(LANES // UNROLL // BLOCK):
                pl.when(h * BLOCK < groups)(functools.partial(block, h))
            return c

        return lax.fori_loop(0, jnp.minimum(CHUNK, deepest - ch * CHUNK), row, c)

    lax.fori_loop(0, chunks, chunk, 0)

    for b in range(nb):
        turned = [
            acc[b * targets + q * LANES : b * targets + (q + 1) * LANES, 0:width].T
            for q in range(8)
        ]
        rest_ref[b] = jnp.concatenate(turned, axis=0)


def gather(feats, front, ids, nbr, wn, ws, dl, second, nb):
    width, verts = feats.shape
    total = nbr.shape[0] * nb * 8
    vmem = pl.BlockSpec(memory_space=pltpu.VMEM)
    return pl.pallas_call(
        functools.partial(gather_kernel, nb),
        out_shape=(
            jax.ShapeDtypeStruct((nb, 8 * width, LANES), F32),
            jax.ShapeDtypeStruct((nb * 8, LANES), jnp.int32),
            jax.ShapeDtypeStruct((1, 8 * LANES), F32),
            jax.ShapeDtypeStruct((2 * width, wn.shape[1]), BF16),
            jax.ShapeDtypeStruct((8, CLASSES + 16), F32),
        ),
        in_specs=[pl.BlockSpec(memory_space=pltpu.HBM)] * 8,
        out_specs=(vmem,) * 5,
        scratch_shapes=[
            pltpu.VMEM((verts + 8, LANES), F32),
            pltpu.VMEM((nb * 8 * LANES + 8, LANES), F32),
            pltpu.VMEM(feats.shape, BF16),
            pltpu.VMEM(ids.shape, jnp.int32),
            pltpu.VMEM(nbr.shape, jnp.int32),
            pltpu.VMEM(wn.shape, BF16),
            pltpu.VMEM(ws.shape, BF16),
            pltpu.VMEM(dl.shape, F32),
            pltpu.VMEM(second.shape, jnp.int32),
            pltpu.VMEM((total + 64, LANES), jnp.int32),
            pltpu.VMEM((total + 64, LANES), jnp.int32),
            pltpu.VMEM((2, CHUNK + 8, LANES), jnp.int32),
            pltpu.SMEM((2 * (CHUNK + 8), LANES), jnp.int32),
            pltpu.SMEM(front.shape, jnp.int32),
            pltpu.SemaphoreType.DMA((2,)),
            pltpu.SemaphoreType.DMA,
            pltpu.SemaphoreType.DMA((7,)),
        ],
        compiler_params=pltpu.CompilerParams(vmem_limit_bytes=VMEM_BYTES),
        cost_estimate=pl.CostEstimate(flops=200000000, bytes_accessed=100000000, transcendentals=0),
        name="neighbour_sums",
    )(feats, front, ids, nbr, wn, ws, dl, second)


def split_dot(ones, wide, dims):
    high = wide.astype(BF16)
    low = (wide - high.astype(F32)).astype(BF16)
    return lax.dot_general(ones, high, dims, preferred_element_type=F32) + lax.dot_general(
        ones, low, dims, preferred_element_type=F32
    )


NN = (((1,), (0,)), ((), ()))
TN = (((0,), (0,)), ((), ()))
NT = (((1,), (1,)), ((), ()))


def layers_kernel(
    nz, ny,
    feats_hbm, front_hbm, rest_hbm, pairs_hbm, deg_hbm, w_hbm, side_hbm,
    b1_hbm, w2s_hbm, w2n_hbm, b2_hbm,
    out_ref,
    feats_ref, table, rest, self_ref, deg_ref, w_ref, side_ref,
    b1_ref, w2s_ref, w2n_ref, b2_ref, load_sems, pairs_s, own_s, sums, part_ref, grads_ref, gotw, sv, sall, got1, xs, got2, pre, got3, lp, got4, l2, got5,
    gp, gotg, gx, gotx, gz, gy,
    sw, rw, sf, rf, sa, ra, sb, rb, s0, r0, s1, r1, s2, r2, s3, r3, s4, r4, s5, r5,
    sg, rg, sz, rz, sy, ry, sx, rx,
):
    feat = lax.axis_index("feat")
    graph = lax.axis_index("graph")
    ng = pairs_hbm.shape[0] // 8
    z = feat // ny
    y = feat % ny
    core = graph % 2
    width = feats_hbm.shape[0]
    fs = front_hbm.shape[0] // ng
    cdim = w2s_ref.shape[0]
    rows = 2 * CLASSES // ng
    nx = ng // 2
    xat = graph // 2

    def at_graph(d):
        return (feat, (graph + d) % ng)

    def at_x(d):
        return (feat, (graph + 2 * d) % ng)

    def at_z(d):
        return (((z + d) % nz) * ny + y, graph)

    def at_y(d):
        return (z * ny + (y + d) % ny, graph)

    sibling = (feat, graph + 1 - 2 * core)

    moved = [
        (feats_hbm, feats_ref), (w_hbm, w_ref), (side_hbm, side_ref),
        (front_hbm.at[pl.ds(pl.multiple_of(graph * fs, fs), 8 * LANES)], own_s), (pairs_hbm, pairs_s), (rest_hbm, rest), (deg_hbm, deg_ref), (b1_hbm, b1_ref),
        (w2s_hbm, w2s_ref), (w2n_hbm, w2n_ref), (b2_hbm, b2_ref),
    ]
    loads = [pltpu.make_async_copy(a, b, load_sems.at[i]) for i, (a, b) in enumerate(moved)]
    for load in loads:
        load.start()

    barrier = pltpu.get_barrier_semaphore()
    for d in range(1, ng):
        pl.semaphore_signal(barrier, inc=1, device_id=at_graph(d), device_id_type=MESH)
    for d in range(1, nz):
        pl.semaphore_signal(barrier, inc=1, device_id=at_z(d), device_id_type=MESH)
    for d in range(1, ny):
        pl.semaphore_signal(barrier, inc=1, device_id=at_y(d), device_id_type=MESH)

    targets = 8 * LANES

    def batch_sums(d):
        b = (graph + d) % ng

        def tile(q, c):
            r = b * 8 + q
            into = pl.multiple_of(q * LANES, LANES)
            for at in range(0, LANES, DENSE):
                words = [pairs_s[r, at + u] for u in range(DENSE)]
                got = [
                    table[pl.ds(w & (WORD - 1), 1), :]
                    + table[pl.ds(w >> WORD_BITS, 1), :]
                    for w in words
                ]
                for u in range(DENSE):
                    sums[pl.ds(into + at + u, 1), :] = got[u]
            return c

        lax.fori_loop(0, 8, tile, 0)
        turned = [sums[q * LANES : (q + 1) * LANES, 0:width].T for q in range(8)]
        part_ref[b] = (jnp.concatenate(turned, axis=0) + rest[b]).astype(BF16)

    loads[0].wait()
    build_table(feats_ref, table)
    for load in loads[1:3]:
        load.wait()
    pl.semaphore_wait(barrier, (ng - 1) + (nz - 1) + (ny - 1))

    def remote(src, dst, ssem, rsem, where):
        return pltpu.make_async_remote_copy(
            src_ref=src, dst_ref=dst, send_sem=ssem, recv_sem=rsem,
            device_id=where, device_id_type=MESH,
        )

    def send(src, dst, ssem, rsem, where):
        copy = remote(src, dst, ssem, rsem, where)
        copy.start()
        return copy

    far = nz // 2

    def weight_copy(k):
        to = ((z + (1 - 2 * core) * k + nz) % nz) * ny + y
        return remote(w_ref, gotw.at[z], sw.at[k], rw.at[k], (to, graph))

    def weight_pass(k):
        block = gotw.at[(z - (1 - 2 * core) * k + nz) % nz]
        return remote(block, block, sf.at[k], rf.at[k], sibling)

    def weight_step(k):
        def step():
            weight_copy(k).wait_recv()
            weight_pass(k).start()

        if k < far:
            step()
        else:
            pl.when(core == 0)(step)

    for k in range(1, far):
        weight_copy(k).start()
    pl.when(core == 0)(lambda: weight_copy(far).start())
    gotw[z] = w_ref[...]

    sv[z] = side_ref[...]

    ca = [send(side_ref, sv.at[z], sa.at[d], ra.at[d], at_z(d)) for d in range(1, nz)]

    for load in loads[3:]:
        load.wait()
    batch_sums(1)
    c1 = []
    for d in range(1, ng):
        c1.append(
            send(part_ref.at[(graph + d) % ng], got1.at[d], s1.at[d], r1.at[d], at_graph(d))
        )
        batch_sums((d + 1) % ng)

    def mine(i, c):
        got = [table[pl.ds(own_s[i * OWN + u], 1), :] for u in range(OWN)]
        for u in range(OWN):
            sums[pl.ds(pl.multiple_of(i * OWN, OWN) + u, 1), :] = got[u]
        return c

    lax.fori_loop(0, targets // OWN, mine, 0)
    for q in range(8):
        self_ref[q] = sums[q * LANES : (q + 1) * LANES, 0:width].T
    c0 = [
        send(
            self_ref.at[(z + d) % nz], got2.at[z, pl.ds(width, width)],
            s0.at[d], r0.at[d], at_z(d),
        )
        for d in range(1, nz)
    ]
    got2[z, width : 2 * width, :] = self_ref[z]

    summed = part_ref[graph].astype(F32)
    for d in range(1, ng):
        c1[d - 1].wait_recv()
        summed = summed + got1[d].astype(F32)
    for q in range(8):
        xs[q] = summed[q * width : (q + 1) * width] / deg_ref[:, q * LANES : (q + 1) * LANES]
    c2 = [
        send(
            xs.at[(z + d) % nz], got2.at[z, pl.ds(0, width)], s2.at[d], r2.at[d], at_z(d)
        )
        for d in range(1, nz)
    ]
    got2[z, 0:width, :] = xs[z]
    for c in ca:
        c.wait_recv()
    cb = [send(sv, sall.at[y], sb.at[d], rb.at[d], at_y(d)) for d in range(1, ny)]
    sall[y] = sv[...]
    for k in range(1, far + 1):
        weight_step(k)

    for c in c0 + c2:
        c.wait_recv()
    x = got2[...].reshape(nz * 2 * width, LANES)
    for k in range(1, far):
        weight_pass(k).wait_recv()
    pl.when(core == 1)(lambda: weight_pass(far).wait_recv())
    w = gotw[...].reshape(nz * 2 * width, w_ref.shape[1])
    high = x.astype(BF16)
    low = (x - high.astype(F32)).astype(BF16)
    part = lax.dot_general(high, w, TN, preferred_element_type=F32) + lax.dot_general(
        low, w, TN, preferred_element_type=F32
    )
    for k in range(ny):
        pre[k] = part[:, k * LANES : (k + 1) * LANES]
    c3 = [
        send(pre.at[(y + d) % ny], got3.at[d], s3.at[d], r3.at[d], at_y(d)) for d in range(1, ny)
    ]

    for c in cb:
        c.wait_recv()
    seeds = ny * nz * 8
    side = sall[...].reshape(seeds, side_ref.shape[1])
    dl = side[:, :CLASSES]
    second = side[:, CLASSES:].astype(jnp.int32)
    taken = lax.broadcasted_iota(jnp.int32, second.shape, 1) < FAN2
    deg2 = jnp.sum(jnp.where((second >= 0) & taken, 1.0, 0.0), axis=1, keepdims=True)
    spot = z * LANES + lax.broadcasted_iota(jnp.int32, (seeds, LANES), 1)
    hits = jnp.zeros((seeds, LANES), F32)
    for k in range(FAN2):
        hits = hits + jnp.where(second[:, k : k + 1] == spot, 1.0, 0.0)
    hits = hits.astype(BF16)
    at = lax.broadcasted_iota(jnp.int32, (seeds, LANES), 0)
    row = ((at // 8) % nz) * (ny * 8) + (at // (8 * nz)) * 8 + at % 8
    same = jnp.where(row == spot, 1.0, 0.0).astype(BF16)

    def exact(wide, ones):
        total = jnp.zeros((wide.shape[1], ones.shape[1]), F32)
        for _ in range(3):
            piece = wide.astype(BF16)
            total = total + lax.dot_general(piece, ones, TN, preferred_element_type=F32)
            wide = wide - piece.astype(F32)
        return total

    cot = jnp.concatenate([exact(dl, same), exact(dl / deg2, hits)], axis=0)
    cot_high = cot.astype(BF16)
    cot_low = (cot - cot_high.astype(F32)).astype(BF16)

    h = pre[y] + b1_ref[y]
    for d in range(1, ny):
        c3[d - 1].wait_recv()
        h = h + got3[d]
    h = jnp.maximum(h, 0.0).astype(BF16)

    g = jnp.dot(cot_high, h, preferred_element_type=F32) + jnp.dot(
        cot_low, h, preferred_element_type=F32
    )
    gp[...] = g.reshape(nx, 2, rows, LANES)
    cg = [send(gp.at[:, 1 - core], gotg, sg.at[0], rg.at[0], sibling)]
    cg[0].wait_recv()
    gx[...] = gp[:, core] + gotg[...]
    for d in range(1, nx):
        cg.append(send(gx.at[(xat + d) % nx], gotx.at[d], sg.at[d], rg.at[d], at_x(d)))

    columns = pl.ds(pl.multiple_of(y * LANES, LANES), LANES)
    zs = lax.dot_general(h, w2s_ref[:, columns], NT, preferred_element_type=F32)
    zn = lax.dot_general(h, w2n_ref[:, columns], NT, preferred_element_type=F32)

    gsum = gx[xat]
    for d in range(1, nx):
        cg[d].wait_recv()
        gsum = gsum + gotx[d]
    gz[z] = gsum
    cz = [send(gz.at[z], gz.at[z], sz.at[d], rz.at[d], at_z(d)) for d in range(1, nz)]

    scores = split_dot(hits, zn, NN) / deg2 + split_dot(same, zs, NN)
    lp[...] = scores.reshape(ny, nz, 8, cdim)
    c4 = [
        send(lp.at[(y + d) % ny], got4.at[d], s4.at[d], r4.at[d], at_y(d)) for d in range(1, ny)
    ]

    for c in cz:
        c.wait_recv()
    whole = gz[0]
    for k in range(1, nz):
        whole = whole + gz[k]
    gy[y] = whole
    cy = [send(gy.at[y], gy.at[y], sy.at[d], ry.at[d], at_y(d)) for d in range(1, ny)]

    lsum = lp[y]
    for d in range(1, ny):
        c4[d - 1].wait_recv()
        lsum = lsum + got4[d]
    l2[...] = lsum
    c5 = [
        send(l2.at[(z + d) % nz], got5.at[d], s5.at[d], r5.at[d], at_z(d)) for d in range(1, nz)
    ]

    for c in cy:
        c.wait_recv()
    grads_ref[graph] = gy[...].reshape(ny * rows, LANES).astype(BF16)
    mine = grads_ref.at[graph]
    cx = [send(mine, mine, sx.at[d], rx.at[d], at_graph(d)) for d in range(1, ng)]

    def emit(k):
        block = grads_ref[k].astype(F32)
        base = pl.multiple_of(k * rows, 8)
        for j in range(ny):
            out_ref[pl.ds(base, rows), j * LANES : (j + 1) * LANES] = block[
                j * rows : (j + 1) * rows
            ]

    emit(graph)
    final = l2[z] + b2_ref[...]
    for d in range(1, nz):
        c5[d - 1].wait_recv()
        final = final + got5[d]
    out_ref[2 * CLASSES : 2 * CLASSES + 8, 0:cdim] = final

    for d in range(1, ng):
        cx[d - 1].wait_recv()
        emit((graph - d + ng) % ng)
    for c in ca + cb + c0 + c1 + c2 + c3 + cg + c4 + cz + c5 + cy + cx:
        c.wait_send()

    for k in range(1, far):
        weight_copy(k).wait_send()
        weight_pass(k).wait_send()

    @pl.when(core == 0)
    def _():
        weight_copy(far).wait_send()
        weight_pass(far).wait_send()


def layers(nz, ny, feats, front, rest, pairs, deg, w, side, b1, w2s, w2n, b2):
    ng = pairs.shape[0] // 8
    width = feats.shape[0]
    rows = 8 * width
    cdim = w2s.shape[0]
    cut = 2 * CLASSES // ng
    vmem = pl.BlockSpec(memory_space=pltpu.VMEM)
    dma = lambda n: pltpu.SemaphoreType.DMA((n,))
    pair = lambda n: [dma(n), dma(n)]
    return pl.pallas_call(
        functools.partial(layers_kernel, nz, ny),
        out_shape=jax.ShapeDtypeStruct((2 * CLASSES + 8, w2s.shape[1]), F32),
        in_specs=[pl.BlockSpec(memory_space=pltpu.HBM)] * 11,
        out_specs=vmem,
        scratch_shapes=[
            pltpu.VMEM(feats.shape, BF16),
            pltpu.VMEM((feats.shape[1] + 8, LANES), F32),
            pltpu.VMEM(rest.shape, F32),
            pltpu.VMEM((8, width, LANES), F32),
            pltpu.VMEM(deg.shape, F32),
            pltpu.VMEM(w.shape, BF16),
            pltpu.VMEM(side.shape, F32),
            pltpu.VMEM(b1.shape, F32),
            pltpu.VMEM(w2s.shape, BF16),
            pltpu.VMEM(w2n.shape, BF16),
            pltpu.VMEM(b2.shape, F32),
            pltpu.SemaphoreType.DMA((11,)),
            pltpu.SMEM(pairs.shape, jnp.int32),
            pltpu.SMEM((8 * LANES,), jnp.int32),
            pltpu.VMEM((8 * LANES, LANES), F32),
            pltpu.VMEM((ng, rows, LANES), BF16),
            pltpu.VMEM((ng, ny * cut, LANES), BF16),
            pltpu.VMEM((nz, 2 * width, w.shape[1]), BF16),
            pltpu.VMEM((nz,) + side.shape, F32),
            pltpu.VMEM((ny, nz) + side.shape, F32),
            pltpu.VMEM((ng, rows, LANES), BF16),
            pltpu.VMEM((8, width, LANES), F32),
            pltpu.VMEM((nz, 2 * width, LANES), F32),
            pltpu.VMEM((ny, LANES, LANES), F32),
            pltpu.VMEM((ny, LANES, LANES), F32),
            pltpu.VMEM((ny, nz, 8, cdim), F32),
            pltpu.VMEM((ny, nz, 8, cdim), F32),
            pltpu.VMEM((nz, 8, cdim), F32),
            pltpu.VMEM((nz, 8, cdim), F32),
            pltpu.VMEM((ng // 2, 2, cut, LANES), F32),
            pltpu.VMEM((ng // 2, cut, LANES), F32),
            pltpu.VMEM((ng // 2, cut, LANES), F32),
            pltpu.VMEM((ng // 2, cut, LANES), F32),
            pltpu.VMEM((nz, cut, LANES), F32),
            pltpu.VMEM((ny, cut, LANES), F32),
        ]
        + pair(nz) + pair(nz) + pair(nz) + pair(ny) + pair(nz) + pair(ng) + pair(nz)
        + pair(ny) + pair(ny) + pair(nz) + pair(ng) + pair(nz) + pair(ny) + pair(ng),
        compiler_params=pltpu.CompilerParams(
            collective_id=0, has_side_effects=True, vmem_limit_bytes=VMEM_BYTES
        ),
        cost_estimate=pl.CostEstimate(flops=300000000, bytes_accessed=10000000, transcendentals=0),
        name="layers",
    )(feats, front, rest, pairs, deg, w, side, b1, w2s, w2n, b2)


def on_device(feats, front_ids, nbr1, nbr2, w1_self, w1_neigh, b1, w2_self, w2_neigh, b2, dlogits):
    nb, targets, fan = nbr1.shape
    width, verts = feats.shape
    hidden, cdim = w2_self.shape
    nz, ny = 8, 4

    front = front_ids.reshape(-1)
    rest, pairs, deg, w, side = gather(
        feats, front, front_ids, nbr1.transpose(2, 0, 1),
        w1_neigh, w1_self,
        dlogits[0], nbr2[0], nb,
    )
    out = layers(
        nz, ny, feats, front, rest, pairs, deg, w, side,
        b1.reshape(ny, 1, LANES), w2_self.T, w2_neigh.T, b2.reshape(1, cdim),
    )
    return (
        out[None, 2 * CLASSES :, :cdim],
        out[:cdim].T,
        out[CLASSES : CLASSES + cdim].T,
    )


def solution(mesh):
    in_specs = (
        P("feat", "graph"),
        P(None, "graph", None),
        P(),
        P("graph", "feat", None),
        P("feat", None),
        P("feat", None),
        P(),
        P(),
        P(),
        P(),
        P("graph", "feat", None),
    )
    out_specs = (P("graph", "feat", None), P(), P())
    return jax.shard_map(
        on_device, mesh=mesh, in_specs=in_specs, out_specs=out_specs, check_vma=False
    )
```

```python
import functools

import jax
import jax.numpy as jnp
from jax import lax
from jax.experimental import pallas as pl
from jax.experimental.pallas import tpu as pltpu
from jax.sharding import PartitionSpec as P

LANES = 128
UNROLL = 4
BLOCK = 8
CHUNK = 32
CLASSES = 160
VMEM_BYTES = 60 * 1024 * 1024
FAN2 = 15
DENSE = 8
OWN = 16
WORD_BITS = 15
WORD = 1 << WORD_BITS
MESH = pl.DeviceIdType.MESH
F32 = jnp.float32
BF16 = jnp.bfloat16
VALID = 1 << 29
RANK_AT = 18


def aligned(index, size):
    return pl.ds(pl.multiple_of(index * size, size), size)


def build_table(feats_ref, table):
    width, verts = feats_ref.shape

    def turn(i, c):
        block = feats_ref[:, aligned(i, LANES)].astype(F32)
        table[aligned(i, LANES), 0:width] = block.T
        return c

    lax.fori_loop(0, verts // LANES, turn, 0, unroll=16)
    table[verts : verts + 8, :] = jnp.zeros((8, LANES), F32)


def gather_kernel(
    nb, feats_hbm, front_ref, ids_hbm, nbr_hbm, wn_hbm, ws_hbm, dl_hbm, second_hbm,
    rest_ref, pairs_v, deg_ref, w_ref, side_ref,
    table, acc, feats_ref, ids_ref, nbr_ref, wn_ref, ws_ref, dl_ref, second_ref, one, two, lists_v, lists_s, front_s,
    sems, front_sem, load_sems,
):
    width = feats_ref.shape[0]
    verts = feats_ref.shape[1]
    fan = nbr_ref.shape[0]
    per = fan * nb
    total = per * 8
    targets = 8 * LANES
    fs = front_ref.shape[0] // nb
    fs_bits = fs.bit_length() - 1
    graph = lax.axis_index("graph")

    load_nbr = pltpu.make_async_copy(nbr_hbm, nbr_ref, load_sems.at[0])
    load_nbr.start()
    load_ids = pltpu.make_async_copy(ids_hbm, ids_ref, load_sems.at[1])
    load_ids.start()
    load_feats = pltpu.make_async_copy(feats_hbm, feats_ref, load_sems.at[2])
    load_feats.start()
    small = [
        pltpu.make_async_copy(a, b, load_sems.at[3 + i])
        for i, (a, b) in enumerate(
            [(wn_hbm, wn_ref), (ws_hbm, ws_ref), (dl_hbm, dl_ref), (second_hbm, second_ref)]
        )
    ]
    for load in small:
        load.start()
    fetch = pltpu.make_async_copy(front_ref, front_s, front_sem)
    fetch.start()

    load_nbr.wait()
    degree = jnp.zeros((1, targets), F32)
    for k in range(fan):
        degree = degree + jnp.where(nbr_ref[k, pl.ds(graph, 1), :] >= 0, 1.0, 0.0)
    deg_ref[...] = degree

    part = (nb, targets)
    start = lax.broadcasted_iota(jnp.int32, part, 0) * fs
    tile = lax.broadcasted_iota(jnp.int32, part, 1) >> 7
    seen = jnp.zeros(part, jnp.int32)
    pair = [jnp.zeros(part, jnp.int32), jnp.zeros(part, jnp.int32)]
    for k in range(fan):
        ids = nbr_ref[k]
        here = (ids >> fs_bits) == graph
        local = ids & (fs - 1)
        for j in range(2):
            pair[j] = jnp.where(here & (seen == j), local, pair[j])
        entry = jnp.where(here & (seen > 1), VALID + (local + start) * 8 + tile, 0)
        for q in range(8):
            one[q * per + k * nb : q * per + (k + 1) * nb, :] = entry[
                :, q * LANES : (q + 1) * LANES
            ]
        seen = seen + jnp.where(here, 1, 0)
    load_ids.wait()
    for q in range(8):
        cut = slice(q * LANES, (q + 1) * LANES)
        found = [jnp.zeros((nb, LANES), jnp.int32), jnp.zeros((nb, LANES), jnp.int32)]
        for k in range(fs // LANES):
            line = ids_ref[:, 0, k * LANES : (k + 1) * LANES]
            for j in range(2):
                at = pair[j][:, cut]
                got = jnp.take_along_axis(line, at & (LANES - 1), axis=1)
                found[j] = jnp.where((at >> 7) == k, got, found[j])
        for j in range(2):
            found[j] = jnp.where(seen[:, cut] > j, found[j], verts)
        word = found[1] * WORD + found[0]
        for b in range(nb):
            pairs_v[b * 8 + q : b * 8 + q + 1, :] = word[b : b + 1]

    below = (
        lax.broadcasted_iota(jnp.int32, (per, per), 0)
        > lax.broadcasted_iota(jnp.int32, (per, per), 1)
    ).astype(F32).astype(BF16)
    lost = jnp.zeros((1, LANES), jnp.int32)
    for q in range(8):
        entry = one[q * per : (q + 1) * per, :]
        gone = jnp.where(entry == 0, 1.0, 0.0)
        before = jnp.dot(below, gone.astype(BF16), preferred_element_type=F32)
        rank = before.astype(jnp.int32) + lost
        one[q * per : (q + 1) * per, :] = jnp.where(entry == 0, 0, entry + rank * (1 << RANK_AT))
        lost = lost + jnp.sum(gone, axis=0, keepdims=True).astype(jnp.int32)
    count = total - lost

    src, dst = one, two
    bits = (total - 1).bit_length()
    block = 64
    for step in range(bits):
        far = 1 << step
        flag = 1 << (RANK_AT + step)
        for at in range(0, total, block):
            stay = src[at : at + block, :]
            have = max(0, min(block, total - at - far))
            kept = jnp.where((stay & flag) != 0, 0, stay)
            if have > 0:
                move = src[at + far : at + far + have, :]
                if have < block:
                    move = jnp.concatenate(
                        [move, jnp.zeros((block - have, LANES), jnp.int32)], axis=0
                    )
                kept = jnp.where((move & flag) != 0, move, kept)
            dst[at : at + block, :] = kept
        src, dst = dst, src

    lane_row = lax.broadcasted_iota(jnp.int32, (LANES, LANES), 1)
    key_row = jnp.broadcast_to(count * LANES, (LANES, LANES)) + lane_row
    key_col = key_row.astype(F32).T
    ahead = jnp.where(key_row.astype(F32) > key_col, 1.0, 0.0)
    place = jnp.sum(ahead, axis=1, keepdims=True).astype(jnp.int32)
    order = jnp.where(place == lane_row, 1.0, 0.0).astype(BF16)

    def shuffle(values):
        got = jnp.dot(values.astype(F32).astype(BF16), order, preferred_element_type=F32)
        return got.astype(jnp.int32)

    wide = jnp.broadcast_to(count, (8, LANES))
    sorted_count = (shuffle(wide // 64) * 64 + shuffle(wide % 64))[0:1]
    lane_id = shuffle(lax.broadcasted_iota(jnp.int32, (8, LANES), 1))[0:1]
    count_col = jnp.broadcast_to(sorted_count.astype(F32), (LANES, LANES)).T
    deepest = jnp.max(count)
    chunks = (deepest + CHUNK - 1) // CHUNK

    def prepare(ch, slot):
        entries = src[aligned(ch, CHUNK), :]
        ident = (entries >> 3) & (nb * fs - 1)
        ident = shuffle(ident >> 8) * 256 + shuffle(ident & 255)
        group = shuffle(entries & 7)
        at_row = ch * CHUNK + lax.broadcasted_iota(jnp.int32, (CHUNK, LANES), 0)
        live = sorted_count > at_row
        goal = (ident >> fs_bits) * targets + group * LANES + lane_id
        word = jnp.where(live, goal * WORD + ident, nb * targets * WORD)
        lists_v[slot, 0:CHUNK, :] = word
        row_at = (ch * CHUNK + lane_row).astype(F32)
        in_row = jnp.sum(jnp.where(count_col > row_at, 1.0, 0.0), axis=0, keepdims=True)
        groups = (in_row.astype(jnp.int32) + (UNROLL - 1)) // UNROLL
        lists_v[slot, CHUNK : CHUNK + 8, :] = jnp.broadcast_to(groups, (8, LANES))

    def transfer(slot):
        return pltpu.make_async_copy(
            lists_v.at[slot],
            lists_s.at[pl.ds(pl.multiple_of(slot * (CHUNK + 8), 8), CHUNK + 8)],
            sems.at[slot],
        )

    @pl.when(chunks > 0)
    def _():
        prepare(0, 0)
        transfer(0).start()

    for load in small:
        load.wait()
    w_ref[...] = jnp.concatenate(
        [wn_ref[...].astype(F32), ws_ref[...].astype(F32)], axis=0
    ).astype(BF16)
    side_ref[...] = jnp.zeros_like(side_ref)
    side_ref[:, 0 : dl_ref.shape[1]] = dl_ref[...]
    side_ref[:, CLASSES : CLASSES + second_ref.shape[1]] = second_ref[...].astype(F32)
    load_feats.wait()

    build_table(feats_ref, table)


    def clear(i, c):
        acc[aligned(i, 8), :] = jnp.zeros((8, LANES), F32)
        return c

    lax.fori_loop(0, acc.shape[0] // 8, clear, 0, unroll=25)

    fetch.wait()

    def chunk(ch, c):
        slot = ch & 1
        base = slot * (CHUNK + 8)
        transfer(slot).wait()

        @pl.when(ch + 1 < chunks)
        def _():
            prepare(ch + 1, 1 - slot)
            transfer(1 - slot).start()

        def row(r, c):
            def group(g):
                words = [lists_s[at, g * UNROLL + u] for u in range(UNROLL)]
                got = [table[pl.ds(front_s[w & (WORD - 1)], 1), :] for w in words]
                goals = [w >> WORD_BITS for w in words]
                old = [acc[pl.ds(a, 1), :] for a in goals]
                for u in range(UNROLL):
                    acc[pl.ds(goals[u], 1), :] = got[u] + old[u]

            groups = lists_s[base + CHUNK, r]
            at = base + r

            def block(h):
                for g in range(h * BLOCK, (h + 1) * BLOCK):
                    group(g)

            for h in range(LANES // UNROLL // BLOCK):
                pl.when(h * BLOCK < groups)(functools.partial(block, h))
            return c

        return lax.fori_loop(0, jnp.minimum(CHUNK, deepest - ch * CHUNK), row, c)

    lax.fori_loop(0, chunks, chunk, 0)

    for b in range(nb):
        turned = [
            acc[b * targets + q * LANES : b * targets + (q + 1) * LANES, 0:width].T
            for q in range(8)
        ]
        rest_ref[b] = jnp.concatenate(turned, axis=0)


def gather(feats, front, ids, nbr, wn, ws, dl, second, nb):
    width, verts = feats.shape
    total = nbr.shape[0] * nb * 8
    vmem = pl.BlockSpec(memory_space=pltpu.VMEM)
    return pl.pallas_call(
        functools.partial(gather_kernel, nb),
        out_shape=(
            jax.ShapeDtypeStruct((nb, 8 * width, LANES), F32),
            jax.ShapeDtypeStruct((nb * 8, LANES), jnp.int32),
            jax.ShapeDtypeStruct((1, 8 * LANES), F32),
            jax.ShapeDtypeStruct((2 * width, wn.shape[1]), BF16),
            jax.ShapeDtypeStruct((8, CLASSES + 16), F32),
        ),
        in_specs=[pl.BlockSpec(memory_space=pltpu.HBM)] * 8,
        out_specs=(vmem,) * 5,
        scratch_shapes=[
            pltpu.VMEM((verts + 8, LANES), F32),
            pltpu.VMEM((nb * 8 * LANES + 8, LANES), F32),
            pltpu.VMEM(feats.shape, BF16),
            pltpu.VMEM(ids.shape, jnp.int32),
            pltpu.VMEM(nbr.shape, jnp.int32),
            pltpu.VMEM(wn.shape, BF16),
            pltpu.VMEM(ws.shape, BF16),
            pltpu.VMEM(dl.shape, F32),
            pltpu.VMEM(second.shape, jnp.int32),
            pltpu.VMEM((total + 64, LANES), jnp.int32),
            pltpu.VMEM((total + 64, LANES), jnp.int32),
            pltpu.VMEM((2, CHUNK + 8, LANES), jnp.int32),
            pltpu.SMEM((2 * (CHUNK + 8), LANES), jnp.int32),
            pltpu.SMEM(front.shape, jnp.int32),
            pltpu.SemaphoreType.DMA((2,)),
            pltpu.SemaphoreType.DMA,
            pltpu.SemaphoreType.DMA((7,)),
        ],
        compiler_params=pltpu.CompilerParams(vmem_limit_bytes=VMEM_BYTES),
        cost_estimate=pl.CostEstimate(flops=200000000, bytes_accessed=100000000, transcendentals=0),
        name="neighbour_sums",
    )(feats, front, ids, nbr, wn, ws, dl, second)


def split_dot(ones, wide, dims):
    high = wide.astype(BF16)
    low = (wide - high.astype(F32)).astype(BF16)
    return lax.dot_general(ones, high, dims, preferred_element_type=F32) + lax.dot_general(
        ones, low, dims, preferred_element_type=F32
    )


NN = (((1,), (0,)), ((), ()))
TN = (((0,), (0,)), ((), ()))
NT = (((1,), (1,)), ((), ()))


def layers_kernel(
    nz, ny,
    feats_hbm, front_hbm, rest_hbm, pairs_hbm, deg_hbm, w_hbm, side_hbm,
    b1_hbm, w2s_hbm, w2n_hbm, b2_hbm,
    out_ref,
    feats_ref, table, rest, self_ref, deg_ref, w_ref, side_ref,
    b1_ref, w2s_ref, w2n_ref, b2_ref, load_sems, pairs_s, own_s, sums, part_ref, grads_ref, gotw, sv, sall, got1, xs, got2, pre, got3, lp, got4, l2, got5,
    gp, gotg, gx, gotx, gz, gy,
    sw, rw, sf, rf, sa, ra, sb, rb, s0, r0, s1, r1, s2, r2, s3, r3, s4, r4, s5, r5,
    sg, rg, sz, rz, sy, ry, sx, rx,
):
    feat = lax.axis_index("feat")
    graph = lax.axis_index("graph")
    ng = pairs_hbm.shape[0] // 8
    z = feat // ny
    y = feat % ny
    core = graph % 2
    width = feats_hbm.shape[0]
    fs = front_hbm.shape[0] // ng
    cdim = w2s_ref.shape[0]
    rows = 2 * CLASSES // ng
    nx = ng // 2
    xat = graph // 2

    def at_graph(d):
        return (feat, (graph + d) % ng)

    def at_x(d):
        return (feat, (graph + 2 * d) % ng)

    def at_z(d):
        return (((z + d) % nz) * ny + y, graph)

    def at_y(d):
        return (z * ny + (y + d) % ny, graph)

    sibling = (feat, graph + 1 - 2 * core)

    moved = [
        (feats_hbm, feats_ref), (w_hbm, w_ref), (side_hbm, side_ref),
        (front_hbm.at[pl.ds(pl.multiple_of(graph * fs, fs), 8 * LANES)], own_s), (pairs_hbm, pairs_s), (rest_hbm, rest), (deg_hbm, deg_ref), (b1_hbm, b1_ref),
        (w2s_hbm, w2s_ref), (w2n_hbm, w2n_ref), (b2_hbm, b2_ref),
    ]
    loads = [pltpu.make_async_copy(a, b, load_sems.at[i]) for i, (a, b) in enumerate(moved)]
    for load in loads:
        load.start()

    barrier = pltpu.get_barrier_semaphore()
    for d in range(1, ng):
        pl.semaphore_signal(barrier, inc=1, device_id=at_graph(d), device_id_type=MESH)
    for d in range(1, nz):
        pl.semaphore_signal(barrier, inc=1, device_id=at_z(d), device_id_type=MESH)
    for d in range(1, ny):
        pl.semaphore_signal(barrier, inc=1, device_id=at_y(d), device_id_type=MESH)

    targets = 8 * LANES

    def batch_sums(d):
        b = (graph + d) % ng

        def tile(q, c):
            r = b * 8 + q
            into = pl.multiple_of(q * LANES, LANES)
            for at in range(0, LANES, DENSE):
                words = [pairs_s[r, at + u] for u in range(DENSE)]
                got = [
                    table[pl.ds(w & (WORD - 1), 1), :]
                    + table[pl.ds(w >> WORD_BITS, 1), :]
                    for w in words
                ]
                for u in range(DENSE):
                    sums[pl.ds(into + at + u, 1), :] = got[u]
            return c

        lax.fori_loop(0, 8, tile, 0)
        turned = [sums[q * LANES : (q + 1) * LANES, 0:width].T for q in range(8)]
        part_ref[b] = (jnp.concatenate(turned, axis=0) + rest[b]).astype(BF16)

    loads[0].wait()
    build_table(feats_ref, table)
    for load in loads[1:3]:
        load.wait()
    pl.semaphore_wait(barrier, (ng - 1) + (nz - 1) + (ny - 1))

    def remote(src, dst, ssem, rsem, where):
        return pltpu.make_async_remote_copy(
            src_ref=src, dst_ref=dst, send_sem=ssem, recv_sem=rsem,
            device_id=where, device_id_type=MESH,
        )

    def send(src, dst, ssem, rsem, where):
        copy = remote(src, dst, ssem, rsem, where)
        copy.start()
        return copy

    far = nz // 2

    def weight_copy(k):
        to = ((z + (1 - 2 * core) * k + nz) % nz) * ny + y
        return remote(w_ref, gotw.at[z], sw.at[k], rw.at[k], (to, graph))

    def weight_pass(k):
        block = gotw.at[(z - (1 - 2 * core) * k + nz) % nz]
        return remote(block, block, sf.at[k], rf.at[k], sibling)

    def weight_step(k):
        def step():
            weight_copy(k).wait_recv()
            weight_pass(k).start()

        if k < far:
            step()
        else:
            pl.when(core == 0)(step)

    for k in range(1, far):
        weight_copy(k).start()
    pl.when(core == 0)(lambda: weight_copy(far).start())
    gotw[z] = w_ref[...]

    sv[z] = side_ref[...]

    ca = [send(side_ref, sv.at[z], sa.at[d], ra.at[d], at_z(d)) for d in range(1, nz)]

    for load in loads[3:]:
        load.wait()
    batch_sums(1)
    c1 = []
    for d in range(1, ng):
        c1.append(
            send(part_ref.at[(graph + d) % ng], got1.at[d], s1.at[d], r1.at[d], at_graph(d))
        )
        batch_sums((d + 1) % ng)
        if d == ng // 2:
            for c in ca:
                c.wait_recv()
            cb = [send(sv, sall.at[y], sb.at[d], rb.at[d], at_y(d)) for d in range(1, ny)]
            sall[y] = sv[...]

    def mine(i, c):
        got = [table[pl.ds(own_s[i * OWN + u], 1), :] for u in range(OWN)]
        for u in range(OWN):
            sums[pl.ds(pl.multiple_of(i * OWN, OWN) + u, 1), :] = got[u]
        return c

    lax.fori_loop(0, targets // OWN, mine, 0)
    for q in range(8):
        self_ref[q] = sums[q * LANES : (q + 1) * LANES, 0:width].T
    c0 = [
        send(
            self_ref.at[(z + d) % nz], got2.at[z, pl.ds(width, width)],
            s0.at[d], r0.at[d], at_z(d),
        )
        for d in range(1, nz)
    ]
    got2[z, width : 2 * width, :] = self_ref[z]

    summed = part_ref[graph].astype(F32)
    for d in range(1, ng):
        c1[d - 1].wait_recv()
        summed = summed + got1[d].astype(F32)
    for q in range(8):
        xs[q] = summed[q * width : (q + 1) * width] / deg_ref[:, q * LANES : (q + 1) * LANES]
    c2 = [
        send(
            xs.at[(z + d) % nz], got2.at[z, pl.ds(0, width)], s2.at[d], r2.at[d], at_z(d)
        )
        for d in range(1, nz)
    ]
    got2[z, 0:width, :] = xs[z]
    for k in range(1, far + 1):
        weight_step(k)

    for c in cb:
        c.wait_recv()
    seeds = ny * nz * 8
    side = sall[...].reshape(seeds, side_ref.shape[1])
    dl = side[:, :CLASSES]
    second = side[:, CLASSES:].astype(jnp.int32)
    taken = lax.broadcasted_iota(jnp.int32, second.shape, 1) < FAN2
    deg2 = jnp.sum(jnp.where((second >= 0) & taken, 1.0, 0.0), axis=1, keepdims=True)
    spot = z * LANES + lax.broadcasted_iota(jnp.int32, (seeds, LANES), 1)
    hits = jnp.zeros((seeds, LANES), F32)
    for k in range(FAN2):
        hits = hits + jnp.where(second[:, k : k + 1] == spot, 1.0, 0.0)
    hits = hits.astype(BF16)
    at = lax.broadcasted_iota(jnp.int32, (seeds, LANES), 0)
    row = ((at // 8) % nz) * (ny * 8) + (at // (8 * nz)) * 8 + at % 8
    same = jnp.where(row == spot, 1.0, 0.0).astype(BF16)

    for c in c0 + c2:
        c.wait_recv()
    x = got2[...].reshape(nz * 2 * width, LANES)
    for k in range(1, far):
        weight_pass(k).wait_recv()
    pl.when(core == 1)(lambda: weight_pass(far).wait_recv())
    w = gotw[...].reshape(nz * 2 * width, w_ref.shape[1])
    high = x.astype(BF16)
    low = (x - high.astype(F32)).astype(BF16)
    part = lax.dot_general(high, w, TN, preferred_element_type=F32) + lax.dot_general(
        low, w, TN, preferred_element_type=F32
    )
    for k in range(ny):
        pre[k] = part[:, k * LANES : (k + 1) * LANES]
    c3 = [
        send(pre.at[(y + d) % ny], got3.at[d], s3.at[d], r3.at[d], at_y(d)) for d in range(1, ny)
    ]

    def exact(wide, ones):
        total = jnp.zeros((wide.shape[1], ones.shape[1]), F32)
        for _ in range(3):
            piece = wide.astype(BF16)
            total = total + lax.dot_general(piece, ones, TN, preferred_element_type=F32)
            wide = wide - piece.astype(F32)
        return total

    cot = jnp.concatenate([exact(dl, same), exact(dl / deg2, hits)], axis=0)
    cot_high = cot.astype(BF16)
    cot_low = (cot - cot_high.astype(F32)).astype(BF16)

    h = pre[y] + b1_ref[y]
    for d in range(1, ny):
        c3[d - 1].wait_recv()
        h = h + got3[d]
    h = jnp.maximum(h, 0.0).astype(BF16)

    g = jnp.dot(cot_high, h, preferred_element_type=F32) + jnp.dot(
        cot_low, h, preferred_element_type=F32
    )
    gp[...] = g.reshape(nx, 2, rows, LANES)
    cg = [send(gp.at[:, 1 - core], gotg, sg.at[0], rg.at[0], sibling)]
    cg[0].wait_recv()
    gx[...] = gp[:, core] + gotg[...]
    for d in range(1, nx):
        cg.append(send(gx.at[(xat + d) % nx], gotx.at[d], sg.at[d], rg.at[d], at_x(d)))

    columns = pl.ds(pl.multiple_of(y * LANES, LANES), LANES)
    zs = lax.dot_general(h, w2s_ref[:, columns], NT, preferred_element_type=F32)
    zn = lax.dot_general(h, w2n_ref[:, columns], NT, preferred_element_type=F32)

    gsum = gx[xat]
    for d in range(1, nx):
        cg[d].wait_recv()
        gsum = gsum + gotx[d]
    gz[z] = gsum
    cz = [send(gz.at[z], gz.at[z], sz.at[d], rz.at[d], at_z(d)) for d in range(1, nz)]

    scores = split_dot(hits, zn, NN) / deg2 + split_dot(same, zs, NN)
    lp[...] = scores.reshape(ny, nz, 8, cdim)
    c4 = [
        send(lp.at[(y + d) % ny], got4.at[d], s4.at[d], r4.at[d], at_y(d)) for d in range(1, ny)
    ]

    for c in cz:
        c.wait_recv()
    whole = gz[0]
    for k in range(1, nz):
        whole = whole + gz[k]
    gy[y] = whole
    cy = [send(gy.at[y], gy.at[y], sy.at[d], ry.at[d], at_y(d)) for d in range(1, ny)]

    lsum = lp[y]
    for d in range(1, ny):
        c4[d - 1].wait_recv()
        lsum = lsum + got4[d]
    l2[...] = lsum
    c5 = [
        send(l2.at[(z + d) % nz], got5.at[d], s5.at[d], r5.at[d], at_z(d)) for d in range(1, nz)
    ]

    for c in cy:
        c.wait_recv()
    grads_ref[graph] = gy[...].reshape(ny * rows, LANES).astype(BF16)
    mine = grads_ref.at[graph]
    cx = [send(mine, mine, sx.at[d], rx.at[d], at_graph(d)) for d in range(1, ng)]

    def emit(k):
        block = grads_ref[k].astype(F32)
        base = pl.multiple_of(k * rows, 8)
        for j in range(ny):
            out_ref[pl.ds(base, rows), j * LANES : (j + 1) * LANES] = block[
                j * rows : (j + 1) * rows
            ]

    emit(graph)
    final = l2[z] + b2_ref[...]
    for d in range(1, nz):
        c5[d - 1].wait_recv()
        final = final + got5[d]
    out_ref[2 * CLASSES : 2 * CLASSES + 8, 0:cdim] = final

    for d in range(1, ng):
        cx[d - 1].wait_recv()
        emit((graph - d + ng) % ng)
    for c in ca + cb + c0 + c1 + c2 + c3 + cg + c4 + cz + c5 + cy + cx:
        c.wait_send()

    for k in range(1, far):
        weight_copy(k).wait_send()
        weight_pass(k).wait_send()

    @pl.when(core == 0)
    def _():
        weight_copy(far).wait_send()
        weight_pass(far).wait_send()


def layers(nz, ny, feats, front, rest, pairs, deg, w, side, b1, w2s, w2n, b2):
    ng = pairs.shape[0] // 8
    width = feats.shape[0]
    rows = 8 * width
    cdim = w2s.shape[0]
    cut = 2 * CLASSES // ng
    vmem = pl.BlockSpec(memory_space=pltpu.VMEM)
    dma = lambda n: pltpu.SemaphoreType.DMA((n,))
    pair = lambda n: [dma(n), dma(n)]
    return pl.pallas_call(
        functools.partial(layers_kernel, nz, ny),
        out_shape=jax.ShapeDtypeStruct((2 * CLASSES + 8, w2s.shape[1]), F32),
        in_specs=[pl.BlockSpec(memory_space=pltpu.HBM)] * 11,
        out_specs=vmem,
        scratch_shapes=[
            pltpu.VMEM(feats.shape, BF16),
            pltpu.VMEM((feats.shape[1] + 8, LANES), F32),
            pltpu.VMEM(rest.shape, F32),
            pltpu.VMEM((8, width, LANES), F32),
            pltpu.VMEM(deg.shape, F32),
            pltpu.VMEM(w.shape, BF16),
            pltpu.VMEM(side.shape, F32),
            pltpu.VMEM(b1.shape, F32),
            pltpu.VMEM(w2s.shape, BF16),
            pltpu.VMEM(w2n.shape, BF16),
            pltpu.VMEM(b2.shape, F32),
            pltpu.SemaphoreType.DMA((11,)),
            pltpu.SMEM(pairs.shape, jnp.int32),
            pltpu.SMEM((8 * LANES,), jnp.int32),
            pltpu.VMEM((8 * LANES, LANES), F32),
            pltpu.VMEM((ng, rows, LANES), BF16),
            pltpu.VMEM((ng, ny * cut, LANES), BF16),
            pltpu.VMEM((nz, 2 * width, w.shape[1]), BF16),
            pltpu.VMEM((nz,) + side.shape, F32),
            pltpu.VMEM((ny, nz) + side.shape, F32),
            pltpu.VMEM((ng, rows, LANES), BF16),
            pltpu.VMEM((8, width, LANES), F32),
            pltpu.VMEM((nz, 2 * width, LANES), F32),
            pltpu.VMEM((ny, LANES, LANES), F32),
            pltpu.VMEM((ny, LANES, LANES), F32),
            pltpu.VMEM((ny, nz, 8, cdim), F32),
            pltpu.VMEM((ny, nz, 8, cdim), F32),
            pltpu.VMEM((nz, 8, cdim), F32),
            pltpu.VMEM((nz, 8, cdim), F32),
            pltpu.VMEM((ng // 2, 2, cut, LANES), F32),
            pltpu.VMEM((ng // 2, cut, LANES), F32),
            pltpu.VMEM((ng // 2, cut, LANES), F32),
            pltpu.VMEM((ng // 2, cut, LANES), F32),
            pltpu.VMEM((nz, cut, LANES), F32),
            pltpu.VMEM((ny, cut, LANES), F32),
        ]
        + pair(nz) + pair(nz) + pair(nz) + pair(ny) + pair(nz) + pair(ng) + pair(nz)
        + pair(ny) + pair(ny) + pair(nz) + pair(ng) + pair(nz) + pair(ny) + pair(ng),
        compiler_params=pltpu.CompilerParams(
            collective_id=0, has_side_effects=True, vmem_limit_bytes=VMEM_BYTES
        ),
        cost_estimate=pl.CostEstimate(flops=300000000, bytes_accessed=10000000, transcendentals=0),
        name="layers",
    )(feats, front, rest, pairs, deg, w, side, b1, w2s, w2n, b2)


def finish_kernel(all_ref, logits_ref, gs_ref, gn_ref):
    cdim = gs_ref.shape[0]
    gs_ref[...] = all_ref[0:cdim, :]
    gn_ref[...] = all_ref[CLASSES : CLASSES + cdim, :]
    logits_ref[0] = all_ref[2 * CLASSES : 2 * CLASSES + 8, 0:cdim]


def finish(out, cdim):
    vmem = pl.BlockSpec(memory_space=pltpu.VMEM)
    grads = jax.ShapeDtypeStruct((cdim, out.shape[1]), F32)
    return pl.pallas_call(
        finish_kernel,
        out_shape=(jax.ShapeDtypeStruct((1, 8, cdim), F32), grads, grads),
        in_specs=[vmem],
        out_specs=(vmem, vmem, vmem),
        compiler_params=pltpu.CompilerParams(vmem_limit_bytes=VMEM_BYTES),
        name="finish",
    )(out)


def on_device(feats, front_ids, nbr1, nbr2, w1_self, w1_neigh, b1, w2_self, w2_neigh, b2, dlogits):
    nb, targets, fan = nbr1.shape
    width, verts = feats.shape
    hidden, cdim = w2_self.shape
    nz, ny = 8, 4

    front = front_ids.reshape(-1)
    rest, pairs, deg, w, side = gather(
        feats, front, front_ids, nbr1.transpose(2, 0, 1),
        w1_neigh, w1_self,
        dlogits[0], nbr2[0], nb,
    )
    out = layers(
        nz, ny, feats, front, rest, pairs, deg, w, side,
        b1.reshape(ny, 1, LANES), w2_self.T, w2_neigh.T, b2.reshape(1, cdim),
    )
    logits, grad_s, grad_n = finish(out, cdim)
    return (logits, grad_s.T, grad_n.T)


def solution(mesh):
    in_specs = (
        P("feat", "graph"),
        P(None, "graph", None),
        P(),
        P("graph", "feat", None),
        P("feat", None),
        P("feat", None),
        P(),
        P(),
        P(),
        P(),
        P("graph", "feat", None),
    )
    out_specs = (P("graph", "feat", None), P(), P())
    return jax.shard_map(
        on_device, mesh=mesh, in_specs=in_specs, out_specs=out_specs, check_vma=False
    )
```
